512 devices in a mesh: azi: 32 (over x, z), axl: 16 (over y, core).
Axes of the slice: x: 4, y: 8, z: 8, core: 2. Of those that a mesh axis runs over, the one named last changes fastest.
Arguments:
- explicit_residual: float32 [5, 512, 64, 128], P(None, 'azi', 'axl'), may hold values from -400 to 400
- diffusion: float32 [3, 512, 64, 128], P(None, 'azi', 'axl'), may hold values from 100 to 10000
- source_rate: float32 [512, 64, 128], P('azi', 'axl'), may hold values from 0.05 to 1
- line_mats: float32 [3, 2, 5, 5], replicated, may hold values from -0.15 to 1.5
Outputs:
- increment: float32 [5, 512, 64, 128], P(None, 'azi', 'axl')
The draws below stay inside these ranges and needn't reach their ends.
All inputs are finite; a program needn't handle non-finite values.
Results may differ from the reference program's by a relative error of at most 0.0003.
Values sent between devices are 32-bit elements; how exact they have to be, the bound alone decides.
A program may use at most 64 MiB of HBM per device.

```python
import math
import jax
import jax.numpy as jnp
from jax import lax

CR = 128
NA = 512
NX = 64


def draw_explicit_residual(key, part):
    key = jax.random.fold_in(key, 11)
    full_shape = (5, NA, NX, CR)
    return 60.0 * jax.random.truncated_normal(key, -6.0, 6.0, full_shape, jnp.float32)


def draw_line_mats(key, part):
    key = jax.random.fold_in(key, 23)
    raw_values = jax.random.uniform(key, (3, 2, 5, 5), jnp.float32, -1.0, 1.0)
    mirrored = 0.5 * (raw_values + jnp.swapaxes(raw_values, 2, 3))
    identity = jnp.eye(5, dtype=jnp.float32)
    convection = 0.15 * mirrored[:, 0]
    reaction = identity * (1.0 + 0.5 * raw_values[:, 1]) + (1.0 - identity) * (0.1 * mirrored[:, 1])
    return jnp.stack([convection, reaction], axis=1)


def steps_of(own_key, dims, pieces, low, largest):
    def one(axis_at, blocks):
        draws = jax.random.uniform(jax.random.fold_in(jax.random.fold_in(own_key, 6), axis_at), (blocks,), jnp.float32, low / len(pieces), largest / len(pieces))
        return jnp.repeat(jnp.exp(draws), dims[axis_at] // blocks).reshape((-1,) + (1,) * (len(dims) - axis_at - 1))

    gain = one(*pieces[0])
    for cut in pieces[1:]:
        gain = gain * one(*cut)
    return gain


def setup_inputs(seed: int = 0) -> dict:
    seeds = jax.random.split(jax.random.key(seed), 5)
    return {
        "explicit_residual": draw_explicit_residual(jax.random.fold_in(seeds[4], 71), 0),
        "diffusion": jnp.clip(jnp.exp(math.log(10000.0) - 4.6051702 * jax.random.uniform(seeds[1], (3, NA, NX, CR), jnp.float32) ** steps_of(seeds[1], (3, NA, NX, CR), ((1, 32), (2, 16)), -0.2, 0.2)), 100.0, 10000.0),
        "source_rate": jnp.clip(jnp.exp(math.log(1.0) - 2.9957323 * jax.random.uniform(seeds[2], (NA, NX, CR), jnp.float32) ** steps_of(seeds[2], (NA, NX, CR), ((0, 32), (1, 16)), -0.2, 0.2)), 0.05, 1.0),
        "line_mats": draw_line_mats(jax.random.fold_in(seeds[4], 71), 0),
    }


def matmul(left_block, right_block):
    return jnp.sum(left_block[:, :, None] * right_block[None, :, :], axis=1)


def eliminate(matrix, right_block):
    order = matrix.shape[0]
    augmented = jnp.concatenate([matrix, right_block], axis=1)
    for column in range(order):
        pivot_row = augmented[column] / augmented[column, column][None]
        augmented = augmented - augmented[:, column][:, None] * pivot_row[None]
        augmented = augmented.at[column].set(pivot_row)
    return augmented[:, order:]


def chain_solve(make_row, row_items, block, columns, breadth):
    def forward(carry, row_item):
        prev_gain, prev_part = carry
        lower_block, middle_block, upper_block, right_block = make_row(row_item)
        pivot_block = middle_block - matmul(lower_block, prev_gain)
        target = right_block - matmul(lower_block, prev_part)
        solved = eliminate(pivot_block, jnp.concatenate([upper_block, target], axis=1))
        gain_block = solved[:, :block]
        part_block = solved[:, block:]
        return (gain_block, part_block), (gain_block, part_block)

    initial = (jnp.zeros((block, block, breadth), jnp.float32), jnp.zeros((block, columns, breadth), jnp.float32))
    _, (gains, parts) = lax.scan(forward, initial, row_items)

    def backward(later_value, row_item):
        gain_block, part_block = row_item
        result = part_block - matmul(gain_block, later_value)
        return result, result

    _, values = lax.scan(backward, jnp.zeros((block, columns, breadth), jnp.float32), (gains, parts), reverse=True)
    return values


def periodic_solve(make_row, row_items, block, columns, breadth):
    first_lower, first_middle, first_upper, first_right = make_row(tuple(part_row[0] for part_row in row_items))
    second_lower = make_row(tuple(part_row[1] for part_row in row_items))[0]
    final_upper = make_row(tuple(part_row[-1] for part_row in row_items))[2]
    row_count = row_items[0].shape[0]
    spikes = jnp.zeros((row_count - 1, block, block, breadth), jnp.float32)
    spikes = spikes.at[0].add(second_lower)
    spikes = spikes.at[row_count - 2].add(final_upper)

    def spiked_row(row_item):
        lower_block, middle_block, upper_block, right_block = make_row(row_item[:-1])
        return lower_block, middle_block, upper_block, jnp.concatenate([right_block, row_item[-1]], axis=1)

    rest_items = tuple(part_row[1:] for part_row in row_items) + (spikes,)
    solved = chain_solve(spiked_row, rest_items, block, columns + block, breadth)
    partial_value = solved[:, :, :columns]
    spread = solved[:, :, columns:]
    matrix = first_middle - matmul(first_upper, spread[0]) - matmul(first_lower, spread[-1])
    target = first_right - matmul(first_upper, partial_value[0]) - matmul(first_lower, partial_value[-1])
    head_value = eliminate(matrix, target)
    tail_values = partial_value - jnp.sum(spread[:, :, :, None] * head_value[None, None], axis=2)
    return jnp.concatenate([head_value[None], tail_values], axis=0)


def operator_row(convection, reaction):
    identity = jnp.eye(5, dtype=jnp.float32)[:, :, None]

    def make_row(row_item):
        face_lo, face_hi, source, right_block = row_item
        lower_block = -face_lo * (identity + convection[:, :, None])
        middle_block = (1.0 + face_lo + face_hi) * identity + source * reaction[:, :, None]
        upper_block = -face_hi * (identity - convection[:, :, None])
        return lower_block, middle_block, upper_block, right_block

    return make_row


def solve_direction(state_field, coefficient, source, convection, reaction, periodic):
    if periodic:
        before = jnp.roll(coefficient, 1, axis=0)
        after = jnp.roll(coefficient, -1, axis=0)
    else:
        zero_row = jnp.zeros_like(coefficient[:1])
        before = jnp.concatenate([zero_row, coefficient[:-1]], axis=0)
        after = jnp.concatenate([coefficient[1:], zero_row], axis=0)
    face_lo = 0.5 * (before + coefficient)
    face_hi = 0.5 * (coefficient + after)
    row_count, outer, inner = coefficient.shape
    group = math.gcd(outer, 16)
    blocks = outer // group
    breadth = group * inner

    def regroup(array):
        return array.reshape(row_count, blocks, group, inner).transpose(1, 0, 2, 3).reshape(blocks, row_count, breadth)

    shaped = state_field.reshape(5, row_count, blocks, group, inner).transpose(2, 1, 0, 3, 4)
    shaped = shaped.reshape(blocks, row_count, 5, 1, breadth)
    make_row = operator_row(convection, reaction)

    def one_block(row_items):
        if periodic:
            return periodic_solve(make_row, row_items, 5, 1, breadth)
        return chain_solve(make_row, row_items, 5, 1, breadth)

    solved = lax.map(one_block, (regroup(face_lo), regroup(face_hi), regroup(source), shaped))
    solved = solved.reshape(blocks, row_count, 5, group, inner).transpose(2, 1, 0, 3, 4)
    return solved.reshape(5, row_count, outer, inner)


def reference(explicit_residual, diffusion, source_rate, line_mats):
    first = solve_direction(explicit_residual, diffusion[0], source_rate, line_mats[0, 0], line_mats[0, 1], True)
    moved = jnp.moveaxis(first, 2, 1)
    second = solve_direction(moved, jnp.moveaxis(diffusion[1], 1, 0), jnp.moveaxis(source_rate, 1, 0), line_mats[1, 0], line_mats[1, 1], False)
    second = jnp.moveaxis(second, 1, 2)
    moved = jnp.moveaxis(second, 3, 1)
    third = solve_direction(moved, jnp.moveaxis(diffusion[2], 2, 0), jnp.moveaxis(source_rate, 2, 0), line_mats[2, 0], line_mats[2, 1], False)
    return jnp.moveaxis(third, 1, 3)
```

```python
import functools

import jax
import jax.numpy as jnp
from jax import lax
from jax.experimental import pallas as pl
from jax.experimental.pallas import tpu as pltpu
from jax.sharding import PartitionSpec as P

N = 5
LOWER, UPPER, RIGHT, DIAG = 0, 5, 10, 11


def lane_index():
    return lax.broadcasted_iota(jnp.int32, (8, 128), 1)


def sub_index():
    return lax.broadcasted_iota(jnp.int32, (8, 128), 0)


def roll(x, shift, axis):
    size = 8 if axis == 0 else 128
    return pltpu.roll(x, shift % size, axis)


def azi_from(x, d):
    if abs(d) >= 8:
        return roll(x, -d // 8, 0)
    moved = roll(x, -16 * d, 1)
    if d > 0:
        return jnp.where(lane_index() >= 128 - 16 * d, roll(moved, -1, 0), moved)
    return jnp.where(lane_index() < -16 * d, roll(moved, 1, 0), moved)


def axl_from(x, d):
    return roll(x, -d, 0)


def rad_from(x, d):
    if abs(d) >= 8:
        return roll(x, 64, 1)
    moved = roll(x, -d, 0)
    crossed = sub_index() >= 8 - d if d > 0 else sub_index() < -d
    return jnp.where(crossed, roll(moved, 64, 1), moved)


def factor(m):
    m = [list(row) for row in m]
    inv = []
    for k in range(N):
        inv.append(1.0 / m[k][k])
        for i in range(k + 1, N):
            m[i][k] = m[i][k] * inv[k]
            for j in range(k + 1, N):
                m[i][j] = m[i][j] - m[i][k] * m[k][j]
    return m, inv


def factored_solve(m, inv, b):
    b = list(b)
    for i in range(N):
        for j in range(i):
            b[i] = b[i] - m[i][j] * b[j]
    for i in reversed(range(N)):
        for j in range(i + 1, N):
            b[i] = b[i] - m[i][j] * b[j]
        b[i] = b[i] * inv[i]
    return b


def times(m, v):
    out = []
    for i in range(N):
        acc = m[i][0] * v[0]
        for j in range(1, N):
            acc = acc + m[i][j] * v[j]
        out.append(acc)
    return out


def add(a, b):
    return [x + y for x, y in zip(a, b)]


def sub(a, b):
    return [x - y for x, y in zip(a, b)]


def solve_lines(fields, mats, direction, hats, rows, face, out, neighbour, shifts, first, last):
    base = direction * 50
    convection = [[mats[base + 5 * i + j] for j in range(N)] for i in range(N)]
    reaction = [[mats[base + 25 + 5 * i + j] for j in range(N)] for i in range(N)]
    plus = [[convection[i][j] + (1.0 if i == j else 0.0) for j in range(N)] for i in range(N)]
    minus = [[(1.0 if i == j else 0.0) - convection[i][j] for j in range(N)] for i in range(N)]

    before = neighbour(fields[5, 7], -1)
    after = neighbour(fields[5, 0], 1)
    if first is not None:
        before = jnp.where(first, 0.0, before)
        after = jnp.where(last, 0.0, after)
    face[0] = 0.5 * (before + fields[5, 0])
    face[8] = 0.5 * (fields[5, 7] + after)
    for r in range(1, 8):
        face[r] = 0.5 * (fields[5, r - 1] + fields[5, r])

    def build(r):
        face_lo, face_hi, source = face[r], face[r + 1], fields[6, r]
        middle = 1.0 + face_lo + face_hi
        link_lo, link_hi = face_lo, face_hi
        if first is not None:
            link_lo = jnp.where(first & (r == 0), 0.0, link_lo)
            link_hi = jnp.where(last & (r == 7), 0.0, link_hi)
        diag = [
            [source * reaction[i][j] + middle if i == j else source * reaction[i][j] for j in range(N)]
            for i in range(N)
        ]
        lower = [[link_lo * plus[i][j] for j in range(N)] for i in range(N)]
        upper = [[link_hi * minus[i][j] for j in range(N)] for i in range(N)]
        return diag, lower, upper, [fields[i, r] for i in range(N)]

    def hat(r, col):
        return [hats[r, col * N + i] for i in range(N)]

    def row_matrix(r, start):
        cols = [[rows[r, (start + j) * N + i] for i in range(N)] for j in range(N)]
        return [[cols[j][i] for j in range(N)] for i in range(N)]

    def put(ref, r, col, values):
        for i in range(N):
            ref[r, col * N + i] = values[i]

    def normalise_built(r):
        diag, lower, upper, right = build(r)
        m, inv = factor(diag)
        for j in range(N):
            put(hats, r, LOWER + j, factored_solve(m, inv, [lower[i][j] for i in range(N)]))
            put(hats, r, UPPER + j, factored_solve(m, inv, [upper[i][j] for i in range(N)]))
        put(hats, r, RIGHT, factored_solve(m, inv, right))

    def normalise(r):
        m, inv = factor(row_matrix(r, DIAG))
        for col in range(11):
            put(hats, r, col, factored_solve(m, inv, [rows[r, col * N + i] for i in range(N)]))

    def combine(r, diag, lower, upper, right, prev, following, want_links=True):
        acc = []
        for j in range(N):
            if want_links:
                put(rows, r, LOWER + j, times(lower, prev(LOWER + j)))
            acc.append(sub([diag[i][j] for i in range(N)], times(lower, prev(UPPER + j))))
        total = add(right, times(lower, prev(RIGHT)))
        for j in range(N):
            if want_links:
                put(rows, r, UPPER + j, times(upper, following(UPPER + j)))
            put(rows, r, DIAG + j, sub(acc[j], times(upper, following(LOWER + j))))
        put(rows, r, RIGHT, add(total, times(upper, following(RIGHT))))

    def combine_rows(r, below, above):
        combine(
            r, row_matrix(r, DIAG), row_matrix(r, LOWER), row_matrix(r, UPPER),
            [rows[r, RIGHT * N + i] for i in range(N)],
            lambda col: hat(below, col), lambda col: hat(above, col),
        )

    def borrow(slot, r):
        def one(q, _):
            hats[slot, q] = neighbour(hats[r, q], 1)
            return 0

        lax.fori_loop(0, 11 * N, one, 0, unroll=11)

    @pl.loop(0, 4)
    def _(k):
        normalise_built(2 * k)

    borrow(8, 0)

    @pl.loop(0, 4)
    def _(k):
        r = 2 * k + 1
        combine(r, *build(r), lambda col: hat(r - 1, col), lambda col: hat(r + 1, col))

    @pl.loop(0, 2)
    def _(k):
        normalise(4 * k + 1)

    borrow(9, 1)

    @pl.loop(0, 2)
    def _(k):
        combine_rows(4 * k + 3, 4 * k + 1, 4 * k + 5)

    normalise(3)
    borrow(11, 3)
    combine_rows(7, 3, 11)

    for d in shifts:
        normalise(7)
        combine(
            7, row_matrix(7, DIAG), row_matrix(7, LOWER), row_matrix(7, UPPER),
            [rows[7, RIGHT * N + i] for i in range(N)],
            lambda col: [neighbour(v, -d) for v in hat(7, col)],
            lambda col: [neighbour(v, d) for v in hat(7, col)],
            want_links=first is None or d != shifts[-1],
        )

    diag = row_matrix(7, DIAG)
    if first is None:
        lower, upper = row_matrix(7, LOWER), row_matrix(7, UPPER)
        diag = [[diag[i][j] - lower[i][j] - upper[i][j] for j in range(N)] for i in range(N)]
    m, inv = factor(diag)
    x7 = factored_solve(m, inv, [rows[7, RIGHT * N + i] for i in range(N)])

    def settle(r, below, above):
        lower = [[hats[r, (LOWER + j) * N + i] for j in range(N)] for i in range(N)]
        upper = [[hats[r, (UPPER + j) * N + i] for j in range(N)] for i in range(N)]
        x = add(add(hat(r, RIGHT), times(lower, below)), times(upper, above))
        for i in range(N):
            out[i, r] = x[i]
        return x

    for i in range(N):
        out[i, 7] = x7[i]
    x_low = [neighbour(v, -1) for v in x7]
    x3 = settle(3, x_low, x7)
    x1 = settle(1, x_low, x3)
    x5 = settle(5, x3, x7)
    settle(0, x_low, x1)
    settle(2, x1, x3)
    settle(4, x3, x5)
    settle(6, x5, x7)


def azimuthal_kernel(mats, fields, out, hats, rows, face):
    solve_lines(
        fields, mats, 0, hats, rows, face, out, azi_from, (1, 2, 4, 8, 16, 32), None, None
    )


def plane_kernel(mats, right, coeffs, out, fields, mid, planes, hats, rows, face):
    for i in range(N):
        fields[i] = right[i]
    fields[5] = coeffs[0]
    fields[6] = coeffs[2]
    solve_lines(
        fields, mats, 1, hats, rows, face, mid, axl_from, (1, 2, 4),
        sub_index() == 0, sub_index() == 7,
    )

    def turned(plane):
        flat = plane.reshape(64, 128).T
        return jnp.concatenate([flat[:64], flat[64:]], axis=1)

    for i in range(N):
        planes[i] = turned(mid[i])
    planes[5] = turned(coeffs[1])
    planes[6] = turned(coeffs[2])
    for i in range(7):
        for r in range(8):
            fields[i, r] = planes[i, pl.ds(r, 8, stride=8), :]
    low_half = lane_index() < 64
    solve_lines(
        fields, mats, 2, hats, rows, face, mid, rad_from, (1, 2, 4, 8),
        (sub_index() == 0) & low_half, (sub_index() == 7) & jnp.logical_not(low_half),
    )
    for i in range(N):
        for r in range(8):
            planes[i, pl.ds(r, 8, stride=8), :] = mid[i, r]
        both = planes[i]
        out[i] = jnp.concatenate([both[:, :64], both[:, 64:]], axis=0).T.reshape(8, 8, 128)


SOLVER_SCRATCH = [
    pltpu.VMEM((12, 55, 8, 128), jnp.float32),
    pltpu.VMEM((8, 80, 8, 128), jnp.float32),
    pltpu.VMEM((9, 8, 128), jnp.float32),
]
IN_VMEM = pl.BlockSpec(memory_space=pltpu.VMEM)
IN_SMEM = pl.BlockSpec(memory_space=pltpu.SMEM)
LIMITS = pltpu.CompilerParams(vmem_limit_bytes=32 * 1024 * 1024)


def solve_azimuthal(mats, fields):
    return pl.pallas_call(
        azimuthal_kernel,
        out_shape=jax.ShapeDtypeStruct((5, 8, 8, 128), jnp.float32),
        in_specs=[IN_SMEM, IN_VMEM],
        out_specs=IN_VMEM,
        scratch_shapes=SOLVER_SCRATCH,
        compiler_params=LIMITS,
        cost_estimate=pl.CostEstimate(flops=40000000, bytes_accessed=400000, transcendentals=0),
    )(mats, fields)


def solve_plane(mats, right, coeffs):
    return pl.pallas_call(
        plane_kernel,
        out_shape=jax.ShapeDtypeStruct((5, 8, 8, 128), jnp.float32),
        in_specs=[IN_SMEM, IN_VMEM, IN_VMEM],
        out_specs=IN_VMEM,
        scratch_shapes=[
            pltpu.VMEM((7, 8, 8, 128), jnp.float32),
            pltpu.VMEM((5, 8, 8, 128), jnp.float32),
            pltpu.VMEM((7, 64, 128), jnp.float32),
        ]
        + SOLVER_SCRATCH,
        compiler_params=LIMITS,
        cost_estimate=pl.CostEstimate(flops=80000000, bytes_accessed=500000, transcendentals=0),
    )(mats, right, coeffs)


def to_plane(block):
    q = block.shape[1]
    moved = lax.all_to_all(block.reshape(16, q * 4, 128), "axl", 0, 0, tiled=True)
    return moved.reshape(8, 2, q, 4, 128).transpose(2, 1, 3, 0, 4).reshape(q, 8, 8, 128)


def from_plane(plane):
    moved = plane.reshape(5, 2, 4, 8, 128).transpose(3, 1, 0, 2, 4).reshape(16, 20, 128)
    moved = lax.all_to_all(moved, "axl", 0, 0, tiled=True)
    return moved.reshape(16, 5, 4, 128).transpose(1, 0, 2, 3)


def body(explicit_residual, diffusion, source_rate, line_mats):
    mats = line_mats.reshape(150)
    coeffs = jnp.stack([diffusion[1], diffusion[2], source_rate], axis=1)
    plane_coeffs = to_plane(coeffs)
    fields = jnp.concatenate([explicit_residual, diffusion[:1], source_rate[None]], axis=0)
    packed = fields.reshape(7, 2, 8, 32, 16).transpose(3, 0, 2, 1, 4).reshape(32, 14, 128)
    lines = lax.all_to_all(packed, "azi", 0, 0, tiled=True)
    lines = lines.reshape(32, 56, 32).transpose(1, 0, 2).reshape(7, 8, 8, 128)
    first = solve_azimuthal(mats, lines)
    packed = first.reshape(40, 32, 32).transpose(1, 0, 2).reshape(32, 10, 128)
    packed = lax.all_to_all(packed, "azi", 0, 0, tiled=True)
    block = packed.reshape(32, 5, 8, 2, 16).transpose(3, 2, 1, 0, 4).reshape(16, 5, 4, 128)
    return from_plane(solve_plane(mats, to_plane(block), plane_coeffs))


def solution(mesh):
    in_specs = (
        P(None, "azi", "axl", None),
        P(None, "azi", "axl", None),
        P("azi", "axl", None),
        P(),
    )
    out_specs = P(None, "azi", "axl", None)
    return jax.shard_map(body, mesh=mesh, in_specs=in_specs, out_specs=out_specs, check_vma=False)
```

```python
import jax
import jax.numpy as jnp
from jax import lax
from jax.experimental import pallas as pl
from jax.experimental.pallas import tpu as pltpu
from jax.sharding import PartitionSpec as P

N = 5
LOWER, UPPER, RIGHT, DIAG = 0, 5, 10, 11


def lane_index():
    return lax.broadcasted_iota(jnp.int32, (8, 128), 1)


def sub_index():
    return lax.broadcasted_iota(jnp.int32, (8, 128), 0)


def roll(x, shift, axis):
    size = 8 if axis == 0 else 128
    return pltpu.roll(x, shift % size, axis)


def azi_from(x, d):
    if abs(d) >= 16:
        return roll(x, -2 * d, 1)
    if d == 1:
        ahead, behind = roll(x, -16, 1), roll(x, 16, 1)
        carried = jnp.where(sub_index() == 7, roll(ahead, -1, 0), roll(behind, -1, 0))
        return jnp.where(lane_index() % 32 < 16, ahead, carried)
    if d == -1:
        ahead, behind = roll(x, -16, 1), roll(x, 16, 1)
        carried = jnp.where(sub_index() == 0, roll(behind, 1, 0), roll(ahead, 1, 0))
        return jnp.where(lane_index() % 32 < 16, carried, behind)
    e = d // 2
    moved = roll(x, -e, 0)
    crossed = sub_index() >= 8 - e if e > 0 else sub_index() < -e
    return jnp.where(crossed, roll(moved, -32 if e > 0 else 32, 1), moved)


def axl_from(x, d):
    return roll(x, -d, 0)


def rad_from(x, d):
    if abs(d) >= 8:
        return roll(x, 64, 1)
    moved = roll(x, -d, 0)
    crossed = sub_index() >= 8 - d if d > 0 else sub_index() < -d
    return jnp.where(crossed, roll(moved, 64, 1), moved)


def factor(m):
    m = [list(row) for row in m]
    inv = []
    for k in range(N):
        inv.append(1.0 / m[k][k])
        for i in range(k + 1, N):
            m[i][k] = m[i][k] * inv[k]
            for j in range(k + 1, N):
                m[i][j] = m[i][j] - m[i][k] * m[k][j]
    return m, inv


def factored_solve(m, inv, b):
    b = list(b)
    for i in range(N):
        for j in range(i):
            b[i] = b[i] - m[i][j] * b[j]
    for i in reversed(range(N)):
        for j in range(i + 1, N):
            b[i] = b[i] - m[i][j] * b[j]
        b[i] = b[i] * inv[i]
    return b


def times(m, v):
    out = []
    for i in range(N):
        acc = m[i][0] * v[0]
        for j in range(1, N):
            acc = acc + m[i][j] * v[j]
        out.append(acc)
    return out


def add(a, b):
    return [x + y for x, y in zip(a, b)]


def sub(a, b):
    return [x - y for x, y in zip(a, b)]


def solve_lines(fields, mats, direction, hats, rows, face, out, neighbour, shifts, first, last):
    base = direction * 50
    convection = [[mats[base + 5 * i + j] for j in range(N)] for i in range(N)]
    reaction = [[mats[base + 25 + 5 * i + j] for j in range(N)] for i in range(N)]
    plus = [[convection[i][j] + (1.0 if i == j else 0.0) for j in range(N)] for i in range(N)]
    minus = [[(1.0 if i == j else 0.0) - convection[i][j] for j in range(N)] for i in range(N)]

    before = neighbour(fields[5, 7], -1)
    after = neighbour(fields[5, 0], 1)
    if first is not None:
        before = jnp.where(first, 0.0, before)
        after = jnp.where(last, 0.0, after)
    face[0] = 0.5 * (before + fields[5, 0])
    face[8] = 0.5 * (fields[5, 7] + after)
    for r in range(1, 8):
        face[r] = 0.5 * (fields[5, r - 1] + fields[5, r])

    def build(r):
        face_lo, face_hi, source = face[r], face[r + 1], fields[6, r]
        middle = 1.0 + face_lo + face_hi
        link_lo, link_hi = face_lo, face_hi
        if first is not None:
            link_lo = jnp.where(first & (r == 0), 0.0, link_lo)
            link_hi = jnp.where(last & (r == 7), 0.0, link_hi)
        diag = [
            [source * reaction[i][j] + middle if i == j else source * reaction[i][j] for j in range(N)]
            for i in range(N)
        ]
        lower = [[link_lo * plus[i][j] for j in range(N)] for i in range(N)]
        upper = [[link_hi * minus[i][j] for j in range(N)] for i in range(N)]
        return diag, lower, upper, [fields[i, r] for i in range(N)]

    def hat(r, col):
        return [hats[r, col * N + i] for i in range(N)]

    def row_matrix(r, start):
        cols = [[rows[r, (start + j) * N + i] for i in range(N)] for j in range(N)]
        return [[cols[j][i] for j in range(N)] for i in range(N)]

    def put(ref, r, col, values):
        for i in range(N):
            ref[r, col * N + i] = values[i]

    def normalise_built(r):
        diag, lower, upper, right = build(r)
        m, inv = factor(diag)
        for j in range(N):
            put(hats, r, LOWER + j, factored_solve(m, inv, [lower[i][j] for i in range(N)]))
            put(hats, r, UPPER + j, factored_solve(m, inv, [upper[i][j] for i in range(N)]))
        put(hats, r, RIGHT, factored_solve(m, inv, right))

    def normalise(r):
        m, inv = factor(row_matrix(r, DIAG))
        for col in range(11):
            put(hats, r, col, factored_solve(m, inv, [rows[r, col * N + i] for i in range(N)]))

    def combine(r, diag, lower, upper, right, prev, following, want_links=True):
        acc = []
        for j in range(N):
            if want_links:
                put(rows, r, LOWER + j, times(lower, prev(LOWER + j)))
            acc.append(sub([diag[i][j] for i in range(N)], times(lower, prev(UPPER + j))))
        total = add(right, times(lower, prev(RIGHT)))
        for j in range(N):
            if want_links:
                put(rows, r, UPPER + j, times(upper, following(UPPER + j)))
            put(rows, r, DIAG + j, sub(acc[j], times(upper, following(LOWER + j))))
        put(rows, r, RIGHT, add(total, times(upper, following(RIGHT))))

    def combine_rows(r, below, above):
        combine(
            r, row_matrix(r, DIAG), row_matrix(r, LOWER), row_matrix(r, UPPER),
            [rows[r, RIGHT * N + i] for i in range(N)],
            lambda col: hat(below, col), lambda col: hat(above, col),
        )

    def borrow(slot, r):
        def one(q, _):
            hats[slot, q] = neighbour(hats[r, q], 1)
            return 0

        lax.fori_loop(0, 11 * N, one, 0, unroll=11)

    @pl.loop(0, 4)
    def _(k):
        normalise_built(2 * k)

    borrow(8, 0)

    @pl.loop(0, 4)
    def _(k):
        r = 2 * k + 1
        combine(r, *build(r), lambda col: hat(r - 1, col), lambda col: hat(r + 1, col))

    @pl.loop(0, 2)
    def _(k):
        normalise(4 * k + 1)

    borrow(9, 1)

    @pl.loop(0, 2)
    def _(k):
        combine_rows(4 * k + 3, 4 * k + 1, 4 * k + 5)

    normalise(3)
    borrow(11, 3)
    combine_rows(7, 3, 11)

    for d in shifts:
        normalise(7)
        combine(
            7, row_matrix(7, DIAG), row_matrix(7, LOWER), row_matrix(7, UPPER),
            [rows[7, RIGHT * N + i] for i in range(N)],
            lambda col: [neighbour(v, -d) for v in hat(7, col)],
            lambda col: [neighbour(v, d) for v in hat(7, col)],
            want_links=first is None or d != shifts[-1],
        )

    diag = row_matrix(7, DIAG)
    if first is None:
        lower, upper = row_matrix(7, LOWER), row_matrix(7, UPPER)
        diag = [[diag[i][j] - lower[i][j] - upper[i][j] for j in range(N)] for i in range(N)]
    m, inv = factor(diag)
    x7 = factored_solve(m, inv, [rows[7, RIGHT * N + i] for i in range(N)])

    def settle(r, below, above):
        lower = [[hats[r, (LOWER + j) * N + i] for j in range(N)] for i in range(N)]
        upper = [[hats[r, (UPPER + j) * N + i] for j in range(N)] for i in range(N)]
        x = add(add(hat(r, RIGHT), times(lower, below)), times(upper, above))
        for i in range(N):
            out[i, r] = x[i]
        return x

    for i in range(N):
        out[i, 7] = x7[i]
    x_low = [neighbour(v, -1) for v in x7]
    x3 = settle(3, x_low, x7)
    x1 = settle(1, x_low, x3)
    x5 = settle(5, x3, x7)
    settle(0, x_low, x1)
    settle(2, x1, x3)
    settle(4, x3, x5)
    settle(6, x5, x7)


def swap_blocks(values):
    values = list(values)
    count = len(values)
    width = 128 // count
    bit = 1
    while bit < count:
        upper = (lane_index() // (bit * width)) % 2 == 1
        for a in range(count):
            if a & bit == 0:
                lo, hi = values[a], values[a | bit]
                values[a] = jnp.where(upper, roll(hi, bit * width, 1), lo)
                values[a | bit] = jnp.where(upper, hi, roll(lo, -bit * width, 1))
        bit *= 2
    return values


class Exchange:
    def __init__(self, axis, count, send, recv, rows, pitch, send_sem, recv_sem):
        self.axis, self.count, self.rows, self.pitch = axis, count, rows, pitch
        self.send, self.recv = send, recv
        self.send_sem, self.recv_sem = send_sem, recv_sem
        self.me = lax.axis_index(axis)

    def slot(self, ref, device):
        return ref.at[pl.ds(pl.multiple_of(device * self.pitch, 8), self.rows)]

    def copy(self, k):
        target = lax.rem(self.me + k, self.count)
        return pltpu.make_async_remote_copy(
            src_ref=self.slot(self.send, target),
            dst_ref=self.slot(self.recv, self.me),
            send_sem=self.send_sem.at[k],
            recv_sem=self.recv_sem.at[k],
            device_id={self.axis: target},
            device_id_type=pl.DeviceIdType.MESH,
        )

    def start(self):
        @pl.loop(1, self.count)
        def _(k):
            self.copy(k).start()

        own = pl.ds(pl.multiple_of(self.me * self.pitch, 8), self.rows)
        self.recv[own, :] = self.send[own, :]

    def wait_recv(self):
        @pl.loop(1, self.count)
        def _(k):
            self.copy(k).wait_recv()

    def wait_send(self):
        @pl.loop(1, self.count)
        def _(k):
            self.copy(k).wait_send()


def kernel(
    mats, explicit, diffusion, source_rate, out,
    tiles, staged, a_send, a_recv, b_send, b_recv, k_send, k_recv, c_send, c_recv, o_send, o_recv,
    fields, mid, planes, hats, rows, face, azi_sems, axl_sems,
):
    barrier = pltpu.get_barrier_semaphore()
    for axis, count in (("azi", 32), ("axl", 16)):
        position = lax.axis_index(axis)

        @pl.loop(1, count)
        def _(k):
            pl.semaphore_signal(
                barrier, inc=1, device_id={axis: lax.rem(position + k, count)},
                device_id_type=pl.DeviceIdType.MESH,
            )

    lines_out = Exchange("azi", 32, a_send, a_recv, 14, 16, azi_sems.at[0], azi_sems.at[1])
    lines_back = Exchange("azi", 32, b_send, b_recv, 10, 16, azi_sems.at[2], azi_sems.at[3])
    coeffs_out = Exchange("axl", 16, k_send, k_recv, 12, 16, axl_sems.at[0], axl_sems.at[1])
    plane_out = Exchange("axl", 16, c_send, c_recv, 20, 24, axl_sems.at[2], axl_sems.at[3])
    plane_back = Exchange("axl", 16, o_send, o_recv, 20, 24, axl_sems.at[4], axl_sems.at[5])

    for f in range(7):
        for m in range(8):
            for half in range(2):
                i = (m % 2) * 8 + half * 4 + m // 2
                part = explicit[f, i] if f < 5 else diffusion[0, i] if f == 5 else source_rate[i]
                tiles[f, m, pl.ds(half * 4, 4), :] = part

    @pl.loop(0, 7)
    def _(f):
        for b, value in enumerate(swap_blocks([tiles[f, m] for m in range(8)])):
            staged[b, pl.ds(pl.multiple_of(f * 8, 8), 8), :] = value

    for b in range(8):
        for j in range(4):
            a_send[pl.ds((j * 8 + b) * 16, 14), :] = staged[b, pl.ds(j, 14, stride=4), :]
    for i in range(16):
        for f, part in enumerate((diffusion[1, i], diffusion[2, i], source_rate[i])):
            k_send[pl.ds(i * 16 + f * 4, 4), :] = part

    pl.semaphore_wait(barrier, 46)
    lines_out.start()
    coeffs_out.start()
    lines_out.wait_recv()

    for f in range(7):
        for half in range(2):
            got = [a_recv[pl.ds(t * 128 + f * 2 + half, 8, stride=16), :] for t in range(4)]
            for k, value in enumerate(swap_blocks(got)):
                fields[f, half * 4 + k] = value

    solve_lines(
        fields, mats, 0, hats, rows, face, mid, azi_from, (1, 2, 4, 8, 16, 32), None, None
    )

    for f in range(5):
        for half in range(2):
            values = swap_blocks([mid[f, half * 4 + k] for k in range(4)])
            for t in range(4):
                b_send[pl.ds(t * 128 + f * 2 + half, 8, stride=16), :] = values[t]
    lines_back.start()
    lines_back.wait_recv()
    for f in range(5):
        for b in range(8):
            for half in range(2):
                tiles[f, b, pl.ds(half * 4, 4), :] = b_recv[
                    pl.ds(b * 16 + f * 2 + half, 4, stride=128), :
                ]

    @pl.loop(0, 5)
    def _(f):
        for m, value in enumerate(swap_blocks([tiles[f, b] for b in range(8)])):
            tiles[f, m] = value

    for f in range(5):
        for m in range(8):
            for half in range(2):
                i = (m % 2) * 8 + half * 4 + m // 2
                c_send[pl.ds(i * 24 + f * 4, 4), :] = tiles[f, m, pl.ds(half * 4, 4), :]
    plane_out.start()

    def axial_rows(r, f, pitch):
        return pl.ds((r // 4) * pitch + f * 4 + r % 4, 8, stride=2 * pitch)

    coeffs_out.wait_recv()
    for r in range(8):
        fields[5, r] = k_recv[axial_rows(r, 0, 16), :]
        fields[6, r] = k_recv[axial_rows(r, 2, 16), :]
    plane_out.wait_recv()
    for r in range(8):
        for f in range(5):
            fields[f, r] = c_recv[axial_rows(r, f, 24), :]
    solve_lines(
        fields, mats, 1, hats, rows, face, mid, axl_from, (1, 2, 4),
        sub_index() == 0, sub_index() == 7,
    )

    def turned(plane):
        flat = plane.reshape(64, 128).T
        return jnp.concatenate([flat[:64], flat[64:]], axis=1)

    planes[6] = turned(fields[6])
    for r in range(8):
        fields[6, r] = k_recv[axial_rows(r, 1, 16), :]
    planes[5] = turned(fields[6])
    for f in range(5):
        planes[f] = turned(mid[f])
    for f in range(7):
        for r in range(8):
            fields[f, r] = planes[f, pl.ds(r, 8, stride=8), :]
    low_half = lane_index() < 64
    solve_lines(
        fields, mats, 2, hats, rows, face, mid, rad_from, (1, 2, 4, 8),
        (sub_index() == 0) & low_half, (sub_index() == 7) & jnp.logical_not(low_half),
    )
    for f in range(5):
        for r in range(8):
            planes[f, pl.ds(r, 8, stride=8), :] = mid[f, r]
        both = planes[f]
        mid[f] = jnp.concatenate([both[:, :64], both[:, 64:]], axis=0).T.reshape(8, 8, 128)
        for r in range(8):
            o_send[axial_rows(r, f, 24), :] = mid[f, r]
    plane_back.start()
    plane_back.wait_recv()
    for f in range(5):
        for i in range(16):
            out[f, i] = o_recv[pl.ds(i * 24 + f * 4, 4), :]
    for exchange in (lines_out, lines_back, coeffs_out, plane_out, plane_back):
        exchange.wait_send()


IN_VMEM = pl.BlockSpec(memory_space=pltpu.VMEM)
IN_SMEM = pl.BlockSpec(memory_space=pltpu.SMEM)


def body(explicit_residual, diffusion, source_rate, line_mats):
    return pl.pallas_call(
        kernel,
        out_shape=jax.ShapeDtypeStruct((5, 16, 4, 128), jnp.float32),
        in_specs=[IN_SMEM, IN_VMEM, IN_VMEM, IN_VMEM],
        out_specs=IN_VMEM,
        scratch_shapes=[
            pltpu.VMEM((7, 8, 8, 128), jnp.float32),
            pltpu.VMEM((8, 64, 128), jnp.float32),
            pltpu.VMEM((512, 128), jnp.float32),
            pltpu.VMEM((512, 128), jnp.float32),
            pltpu.VMEM((512, 128), jnp.float32),
            pltpu.VMEM((512, 128), jnp.float32),
            pltpu.VMEM((256, 128), jnp.float32),
            pltpu.VMEM((256, 128), jnp.float32),
            pltpu.VMEM((384, 128), jnp.float32),
            pltpu.VMEM((384, 128), jnp.float32),
            pltpu.VMEM((384, 128), jnp.float32),
            pltpu.VMEM((384, 128), jnp.float32),
            pltpu.VMEM((7, 8, 8, 128), jnp.float32),
            pltpu.VMEM((5, 8, 8, 128), jnp.float32),
            pltpu.VMEM((7, 64, 128), jnp.float32),
            pltpu.VMEM((12, 55, 8, 128), jnp.float32),
            pltpu.VMEM((8, 80, 8, 128), jnp.float32),
            pltpu.VMEM((9, 8, 128), jnp.float32),
            pltpu.SemaphoreType.DMA((4, 32)),
            pltpu.SemaphoreType.DMA((6, 16)),
        ],
        compiler_params=pltpu.CompilerParams(
            collective_id=0, has_side_effects=True, vmem_limit_bytes=32 * 1024 * 1024
        ),
        cost_estimate=pl.CostEstimate(
            flops=120000000, bytes_accessed=600000, transcendentals=0
        ),
    )(line_mats.reshape(150), explicit_residual, diffusion, source_rate)


def solution(mesh):
    in_specs = (
        P(None, "azi", "axl", None),
        P(None, "azi", "axl", None),
        P("azi", "axl", None),
        P(),
    )
    out_specs = P(None, "azi", "axl", None)
    return jax.shard_map(body, mesh=mesh, in_specs=in_specs, out_specs=out_specs, check_vma=False)
```

```python
import jax
import jax.numpy as jnp
from jax import lax
from jax.experimental import pallas as pl
from jax.experimental.pallas import tpu as pltpu
from jax.sharding import PartitionSpec as P

N = 5
LOWER, UPPER, DIAG = 0, 5, 10


def lane_index():
    return lax.broadcasted_iota(jnp.int32, (8, 128), 1)


def sub_index():
    return lax.broadcasted_iota(jnp.int32, (8, 128), 0)


def roll(x, shift, axis):
    size = 8 if axis == 0 else 128
    return pltpu.roll(x, shift % size, axis)


def azi_from(x, d):
    if abs(d) >= 16:
        return roll(x, -2 * d, 1)
    if d == 1:
        ahead, behind = roll(x, -16, 1), roll(x, 16, 1)
        carried = jnp.where(sub_index() == 7, roll(ahead, -1, 0), roll(behind, -1, 0))
        return jnp.where(lane_index() % 32 < 16, ahead, carried)
    if d == -1:
        ahead, behind = roll(x, -16, 1), roll(x, 16, 1)
        carried = jnp.where(sub_index() == 0, roll(behind, 1, 0), roll(ahead, 1, 0))
        return jnp.where(lane_index() % 32 < 16, carried, behind)
    e = d // 2
    moved = roll(x, -e, 0)
    crossed = sub_index() >= 8 - e if e > 0 else sub_index() < -e
    return jnp.where(crossed, roll(moved, -32 if e > 0 else 32, 1), moved)


def axl_from(x, d):
    return roll(x, -d, 0)


def rad_from(x, d):
    if abs(d) >= 8:
        return roll(x, 64, 1)
    moved = roll(x, -d, 0)
    crossed = sub_index() >= 8 - d if d > 0 else sub_index() < -d
    return jnp.where(crossed, roll(moved, 64, 1), moved)


def factor(m):
    m = [list(row) for row in m]
    inv = []
    for k in range(N):
        inv.append(1.0 / m[k][k])
        for i in range(k + 1, N):
            m[i][k] = m[i][k] * inv[k]
            for j in range(k + 1, N):
                m[i][j] = m[i][j] - m[i][k] * m[k][j]
    return m, inv


def factored_solve(m, inv, b):
    b = list(b)
    for i in range(N):
        for j in range(i):
            b[i] = b[i] - m[i][j] * b[j]
    for i in reversed(range(N)):
        for j in range(i + 1, N):
            b[i] = b[i] - m[i][j] * b[j]
        b[i] = b[i] * inv[i]
    return b


def times(m, v):
    out = []
    for i in range(N):
        acc = m[i][0] * v[0]
        for j in range(1, N):
            acc = acc + m[i][j] * v[j]
        out.append(acc)
    return out


def add(a, b):
    return [x + y for x, y in zip(a, b)]


def sub(a, b):
    return [x - y for x, y in zip(a, b)]


class LineSolver:
    def __init__(self, mats, direction, neighbour, shifts, first, last, store):
        self.hats, self.links, self.factors, self.face = store
        self.neighbour, self.shifts, self.first, self.last = neighbour, shifts, first, last
        base = direction * 50
        convection = [[mats[base + 5 * i + j] for j in range(N)] for i in range(N)]
        self.reaction = [[mats[base + 25 + 5 * i + j] for j in range(N)] for i in range(N)]
        unit = [[1.0 if i == j else 0.0 for j in range(N)] for i in range(N)]
        self.plus = [[unit[i][j] + convection[i][j] for j in range(N)] for i in range(N)]
        self.minus = [[unit[i][j] - convection[i][j] for j in range(N)] for i in range(N)]

    def built_links(self, r):
        link_lo, link_hi = self.face[r], self.face[r + 1]
        if self.first is not None:
            link_lo = jnp.where(self.first & (r == 0), 0.0, link_lo)
            link_hi = jnp.where(self.last & (r == 7), 0.0, link_hi)
        lower = [[link_lo * self.plus[i][j] for j in range(N)] for i in range(N)]
        upper = [[link_hi * self.minus[i][j] for j in range(N)] for i in range(N)]
        return lower, upper

    def built_diag(self, r, source):
        middle = 1.0 + self.face[r] + self.face[r + 1]
        return [
            [
                source * self.reaction[i][j] + middle if i == j else source * self.reaction[i][j]
                for j in range(N)
            ]
            for i in range(N)
        ]

    def matrix(self, ref, slot, start):
        cols = [[ref[slot, (start + j) * N + i] for i in range(N)] for j in range(N)]
        return [[cols[j][i] for j in range(N)] for i in range(N)]

    def put(self, ref, slot, col, values):
        for i in range(N):
            ref[slot, col * N + i] = values[i]

    def keep_factor(self, slot, diag):
        m, inv = factor(diag)
        for i in range(N):
            for j in range(N):
                self.factors[slot, i * N + j] = inv[i] if i == j else m[i][j]
        return m, inv

    def solved(self, slot, right):
        m = [[self.factors[slot, i * N + j] for j in range(N)] for i in range(N)]
        return factored_solve(m, [m[i][i] for i in range(N)], right)

    def hat_column(self, slot, col):
        return [self.hats[slot, col * N + i] for i in range(N)]

    def prepare(self, coeff, source):
        neighbour, face, first = self.neighbour, self.face, self.first
        hats, links = self.hats, self.links
        before, after = neighbour(coeff[7], -1), neighbour(coeff[0], 1)
        if first is not None:
            before = jnp.where(first, 0.0, before)
            after = jnp.where(self.last, 0.0, after)
        face[0] = 0.5 * (before + coeff[0])
        face[8] = 0.5 * (coeff[7] + after)
        for r in range(1, 8):
            face[r] = 0.5 * (coeff[r - 1] + coeff[r])

        def normalise(slot, kept, diag, column):
            m, inv = self.keep_factor(kept, diag)
            for col in range(10):
                self.put(hats, slot, col, factored_solve(m, inv, column(col)))

        def normalise_built(r, kept):
            lower, upper = self.built_links(r)
            both = [lower, upper]
            normalise(
                r, kept, self.built_diag(r, source[r]),
                lambda col: [both[col // N][i][col % N] for i in range(N)],
            )

        def normalise_kept(slot, row, kept):
            normalise(
                slot, kept, self.matrix(links, row, DIAG),
                lambda col: [links[row, col * N + i] for i in range(N)],
            )

        def combine(target, diag, lower, upper, prev, following, want_links=True):
            acc = []
            for j in range(N):
                if want_links:
                    self.put(links, target, LOWER + j, times(lower, prev(LOWER + j)))
                acc.append(sub([diag[i][j] for i in range(N)], times(lower, prev(UPPER + j))))
            for j in range(N):
                if want_links:
                    self.put(links, target, UPPER + j, times(upper, following(UPPER + j)))
                self.put(
                    links, target, DIAG + j, sub(acc[j], times(upper, following(LOWER + j)))
                )

        def combine_kept(target, row, below, above):
            combine(
                target, self.matrix(links, row, DIAG), self.matrix(links, row, LOWER),
                self.matrix(links, row, UPPER), lambda col: self.hat_column(below, col),
                lambda col: self.hat_column(above, col),
            )

        def borrow(slot, r):
            def one(q, _):
                hats[slot, q] = neighbour(hats[r, q], 1)
                return 0

            lax.fori_loop(0, 10 * N, one, 0, unroll=10)

        @pl.loop(0, 4)
        def _(k):
            normalise_built(2 * k, k)

        borrow(8, 0)

        @pl.loop(0, 4)
        def _(k):
            r = 2 * k + 1
            lower, upper = self.built_links(r)
            combine(
                r, self.built_diag(r, source[r]), lower, upper,
                lambda col: self.hat_column(r - 1, col), lambda col: self.hat_column(r + 1, col),
            )

        @pl.loop(0, 2)
        def _(k):
            normalise_kept(4 * k + 1, 4 * k + 1, 4 + k)

        borrow(9, 1)

        @pl.loop(0, 2)
        def _(k):
            combine_kept(8 + k, 4 * k + 3, 4 * k + 1, 4 * k + 5)

        normalise_kept(3, 8, 6)
        borrow(11, 3)
        combine_kept(10, 9, 3, 11)
        for k, d in enumerate(self.shifts):
            row = 10 + k
            normalise_kept(7, row, 7 + k)
            combine(
                row + 1, self.matrix(links, row, DIAG), self.matrix(links, row, LOWER),
                self.matrix(links, row, UPPER),
                lambda col: [neighbour(v, -d) for v in self.hat_column(7, col)],
                lambda col: [neighbour(v, d) for v in self.hat_column(7, col)],
                want_links=first is None or d != self.shifts[-1],
            )
        row = 10 + len(self.shifts)
        diag = self.matrix(links, row, DIAG)
        if first is None:
            lower, upper = self.matrix(links, row, LOWER), self.matrix(links, row, UPPER)
            diag = [[diag[i][j] - lower[i][j] - upper[i][j] for j in range(N)] for i in range(N)]
        self.keep_factor(7 + len(self.shifts), diag)

    def finish(self, right, out):
        neighbour, links = self.neighbour, self.links

        def gather(r, lower, upper, below, above):
            return add(add(r, times(lower, below)), times(upper, above))

        def kept(row):
            return self.matrix(links, row, LOWER), self.matrix(links, row, UPPER)

        def shifted(values, d):
            return [neighbour(v, d) for v in values]

        def load(r):
            return [right[i, r] for i in range(N)]

        hat = {r: self.solved(r // 2, load(r)) for r in (0, 2, 4, 6)}
        hat[8] = shifted(hat[0], 1)
        rhs = {
            r: gather(load(r), *self.built_links(r), hat[r - 1], hat[r + 1]) for r in (1, 3, 5, 7)
        }
        hat[1], hat[5] = self.solved(4, rhs[1]), self.solved(5, rhs[5])
        rhs[3] = gather(rhs[3], *kept(3), hat[1], hat[5])
        rhs[7] = gather(rhs[7], *kept(7), hat[5], shifted(hat[1], 1))
        hat[3] = self.solved(6, rhs[3])
        last = gather(rhs[7], *kept(9), hat[3], shifted(hat[3], 1))
        for k, d in enumerate(self.shifts):
            part = self.solved(7 + k, last)
            last = gather(last, *kept(10 + k), shifted(part, -d), shifted(part, d))
        x = {7: self.solved(7 + len(self.shifts), last)}
        x[-1] = shifted(x[7], -1)

        def settle(r, step):
            lower = self.matrix(self.hats, r, LOWER)
            upper = self.matrix(self.hats, r, UPPER)
            x[r] = gather(hat[r], lower, upper, x[r - step], x[r + step])

        for r, step in ((3, 4), (1, 2), (5, 2), (0, 1), (2, 1), (4, 1), (6, 1)):
            settle(r, step)
        for r in range(8):
            for i in range(N):
                out[i, r] = x[r][i]


def swap_blocks(values):
    values = list(values)
    count = len(values)
    width = 128 // count
    bit = 1
    while bit < count:
        upper = (lane_index() // (bit * width)) % 2 == 1
        for a in range(count):
            if a & bit == 0:
                lo, hi = values[a], values[a | bit]
                values[a] = jnp.where(upper, roll(hi, bit * width, 1), lo)
                values[a | bit] = jnp.where(upper, hi, roll(lo, -bit * width, 1))
        bit *= 2
    return values


class Exchange:
    def __init__(self, axis, count, send, recv, start, rows, pitch, send_sem, recv_sem):
        self.axis, self.count, self.offset = axis, count, start
        self.rows, self.pitch = rows, pitch
        self.send, self.recv = send, recv
        self.send_sem, self.recv_sem = send_sem, recv_sem
        self.me = lax.axis_index(axis)

    def slot(self, ref, device):
        return ref.at[pl.ds(pl.multiple_of(device * self.pitch + self.offset, 8), self.rows)]

    def copy(self, k):
        target = lax.rem(self.me + k, self.count)
        return pltpu.make_async_remote_copy(
            src_ref=self.slot(self.send, target),
            dst_ref=self.slot(self.recv, self.me),
            send_sem=self.send_sem.at[k],
            recv_sem=self.recv_sem.at[k],
            device_id={self.axis: target},
            device_id_type=pl.DeviceIdType.MESH,
        )

    def start(self):
        @pl.loop(1, self.count)
        def _(k):
            self.copy(k).start()

        own = pl.ds(pl.multiple_of(self.me * self.pitch + self.offset, 8), self.rows)
        self.recv[own, :] = self.send[own, :]

    def wait_recv(self):
        @pl.loop(1, self.count)
        def _(k):
            self.copy(k).wait_recv()

    def wait_send(self):
        @pl.loop(1, self.count)
        def _(k):
            self.copy(k).wait_send()


def kernel(
    mats, explicit, diffusion, source_rate, out,
    tiles, staged, a_send, a_recv, b_send, b_recv, k_send, k_recv, c_send, c_recv, o_send, o_recv,
    fields, mid, planes, hats, links, factors, face, azi_sems, axl_sems,
):
    barrier = pltpu.get_barrier_semaphore()
    for axis, count in (("azi", 32), ("axl", 16)):
        position = lax.axis_index(axis)

        @pl.loop(1, count)
        def _(k):
            pl.semaphore_signal(
                barrier, inc=1, device_id={axis: lax.rem(position + k, count)},
                device_id_type=pl.DeviceIdType.MESH,
            )

    lines_coeffs = Exchange("azi", 32, a_send, a_recv, 0, 4, 24, azi_sems.at[4], azi_sems.at[5])
    lines_out = Exchange("azi", 32, a_send, a_recv, 8, 10, 24, azi_sems.at[0], azi_sems.at[1])
    lines_back = Exchange("azi", 32, b_send, b_recv, 0, 10, 16, azi_sems.at[2], azi_sems.at[3])
    coeffs_out = Exchange("axl", 16, k_send, k_recv, 0, 12, 16, axl_sems.at[0], axl_sems.at[1])
    plane_out = Exchange("axl", 16, c_send, c_recv, 0, 20, 24, axl_sems.at[2], axl_sems.at[3])
    plane_back = Exchange("axl", 16, o_send, o_recv, 0, 20, 24, axl_sems.at[4], axl_sems.at[5])

    low_half = lane_index() < 64

    def store(k):
        return hats.at[k], links.at[k], factors.at[k], face.at[k]

    azimuthal = LineSolver(mats, 0, azi_from, (1, 2, 4, 8, 16, 32), None, None, store(0))
    axial = LineSolver(
        mats, 1, axl_from, (1, 2, 4), sub_index() == 0, sub_index() == 7, store(1)
    )
    radial = LineSolver(
        mats, 2, rad_from, (1, 2, 4, 8), (sub_index() == 0) & low_half,
        (sub_index() == 7) & jnp.logical_not(low_half), store(0),
    )

    def stage(f, place, part):
        for m in range(8):
            for half in range(2):
                i = (m % 2) * 8 + half * 4 + m // 2
                tiles[f, m, pl.ds(half * 4, 4), :] = part(i)
        for b, value in enumerate(swap_blocks([tiles[f, m] for m in range(8)])):
            staged[b, pl.ds(place, 8), :] = value

    stage(5, 0, lambda i: diffusion[0, i])
    stage(6, 8, lambda i: source_rate[i])
    for b in range(8):
        for j in range(4):
            a_send[pl.ds((j * 8 + b) * 24, 4), :] = staged[b, pl.ds(j, 4, stride=4), :]

    pl.semaphore_wait(barrier, 46)
    lines_coeffs.start()

    for f in range(5):
        stage(f, 16 + f * 8, lambda i: explicit[f, i])
    for b in range(8):
        for j in range(4):
            a_send[pl.ds((j * 8 + b) * 24 + 8, 10), :] = staged[b, pl.ds(16 + j, 10, stride=4), :]
    lines_out.start()

    for i in range(16):
        for f, part in enumerate((diffusion[1, i], diffusion[2, i], source_rate[i])):
            k_send[pl.ds(i * 16 + f * 4, 4), :] = part
    coeffs_out.start()

    def take_lines(f, row):
        for half in range(2):
            got = [a_recv[pl.ds(t * 192 + row + half, 8, stride=24), :] for t in range(4)]
            for k, value in enumerate(swap_blocks(got)):
                fields[f, half * 4 + k] = value

    lines_coeffs.wait_recv()
    take_lines(5, 0)
    take_lines(6, 2)
    azimuthal.prepare(fields.at[5], fields.at[6])
    lines_out.wait_recv()
    for f in range(5):
        take_lines(f, 8 + 2 * f)
    azimuthal.finish(fields, mid)

    for f in range(5):
        for half in range(2):
            values = swap_blocks([mid[f, half * 4 + k] for k in range(4)])
            for t in range(4):
                b_send[pl.ds(t * 128 + f * 2 + half, 8, stride=16), :] = values[t]
    lines_back.start()

    def axial_rows(r, f, pitch):
        return pl.ds((r // 4) * pitch + f * 4 + r % 4, 8, stride=2 * pitch)

    coeffs_out.wait_recv()
    for r in range(8):
        fields[5, r] = k_recv[axial_rows(r, 0, 16), :]
        fields[6, r] = k_recv[axial_rows(r, 2, 16), :]
    axial.prepare(fields.at[5], fields.at[6])

    lines_back.wait_recv()
    for f in range(5):
        for b in range(8):
            for half in range(2):
                tiles[f, b, pl.ds(half * 4, 4), :] = b_recv[
                    pl.ds(b * 16 + f * 2 + half, 4, stride=128), :
                ]
        for m, value in enumerate(swap_blocks([tiles[f, b] for b in range(8)])):
            tiles[f, m] = value
        for m in range(8):
            for half in range(2):
                i = (m % 2) * 8 + half * 4 + m // 2
                c_send[pl.ds(i * 24 + f * 4, 4), :] = tiles[f, m, pl.ds(half * 4, 4), :]
    plane_out.start()

    def turned(plane):
        flat = plane.reshape(64, 128).T
        return jnp.concatenate([flat[:64], flat[64:]], axis=1)

    def turn_rows(f):
        for r in range(8):
            fields[f, r] = planes[f, pl.ds(r, 8, stride=8), :]

    planes[6] = turned(fields[6])
    for r in range(8):
        fields[5, r] = k_recv[axial_rows(r, 1, 16), :]
    planes[5] = turned(fields[5])
    turn_rows(5)
    turn_rows(6)
    radial.prepare(fields.at[5], fields.at[6])

    plane_out.wait_recv()
    for r in range(8):
        for f in range(5):
            fields[f, r] = c_recv[axial_rows(r, f, 24), :]
    axial.finish(fields, mid)
    for f in range(5):
        planes[f] = turned(mid[f])
        turn_rows(f)
    radial.finish(fields, mid)
    for f in range(5):
        for r in range(8):
            planes[f, pl.ds(r, 8, stride=8), :] = mid[f, r]
        both = planes[f]
        mid[f] = jnp.concatenate([both[:, :64], both[:, 64:]], axis=0).T.reshape(8, 8, 128)
        for r in range(8):
            o_send[axial_rows(r, f, 24), :] = mid[f, r]
    plane_back.start()
    plane_back.wait_recv()
    for f in range(5):
        for i in range(16):
            out[f, i] = o_recv[pl.ds(i * 24 + f * 4, 4), :]
    for exchange in (lines_coeffs, lines_out, lines_back, coeffs_out, plane_out, plane_back):
        exchange.wait_send()


IN_VMEM = pl.BlockSpec(memory_space=pltpu.VMEM)
IN_SMEM = pl.BlockSpec(memory_space=pltpu.SMEM)


def body(explicit_residual, diffusion, source_rate, line_mats):
    return pl.pallas_call(
        kernel,
        out_shape=jax.ShapeDtypeStruct((5, 16, 4, 128), jnp.float32),
        in_specs=[IN_SMEM, IN_VMEM, IN_VMEM, IN_VMEM],
        out_specs=IN_VMEM,
        scratch_shapes=[
            pltpu.VMEM((7, 8, 8, 128), jnp.float32),
            pltpu.VMEM((8, 64, 128), jnp.float32),
            pltpu.VMEM((768, 128), jnp.float32),
            pltpu.VMEM((768, 128), jnp.float32),
            pltpu.VMEM((512, 128), jnp.float32),
            pltpu.VMEM((512, 128), jnp.float32),
            pltpu.VMEM((256, 128), jnp.float32),
            pltpu.VMEM((256, 128), jnp.float32),
            pltpu.VMEM((384, 128), jnp.float32),
            pltpu.VMEM((384, 128), jnp.float32),
            pltpu.VMEM((384, 128), jnp.float32),
            pltpu.VMEM((384, 128), jnp.float32),
            pltpu.VMEM((7, 8, 8, 128), jnp.float32),
            pltpu.VMEM((5, 8, 8, 128), jnp.float32),
            pltpu.VMEM((7, 64, 128), jnp.float32),
            pltpu.VMEM((2, 12, 50, 8, 128), jnp.float32),
            pltpu.VMEM((2, 17, 75, 8, 128), jnp.float32),
            pltpu.VMEM((2, 14, 25, 8, 128), jnp.float32),
            pltpu.VMEM((2, 9, 8, 128), jnp.float32),
            pltpu.SemaphoreType.DMA((6, 32)),
            pltpu.SemaphoreType.DMA((6, 16)),
        ],
        compiler_params=pltpu.CompilerParams(
            collective_id=0, has_side_effects=True, vmem_limit_bytes=32 * 1024 * 1024
        ),
        cost_estimate=pl.CostEstimate(
            flops=120000000, bytes_accessed=600000, transcendentals=0
        ),
    )(line_mats.reshape(150), explicit_residual, diffusion, source_rate)


def solution(mesh):
    in_specs = (
        P(None, "azi", "axl", None),
        P(None, "azi", "axl", None),
        P("azi", "axl", None),
        P(),
    )
    out_specs = P(None, "azi", "axl", None)
    return jax.shard_map(body, mesh=mesh, in_specs=in_specs, out_specs=out_specs, check_vma=False)
```

```python
import jax
import jax.numpy as jnp
from jax import lax
from jax.experimental import pallas as pl
from jax.experimental.pallas import tpu as pltpu
from jax.sharding import PartitionSpec as P

N = 5
LOWER, UPPER, DIAG = 0, 5, 10


def lane_index():
    return lax.broadcasted_iota(jnp.int32, (8, 128), 1)


def sub_index():
    return lax.broadcasted_iota(jnp.int32, (8, 128), 0)


def roll(x, shift, axis):
    size = 8 if axis == 0 else 128
    return pltpu.roll(x, shift % size, axis)


def azi_from(x, d):
    if abs(d) >= 16:
        return roll(x, -2 * d, 1)
    if d == 1:
        ahead, behind = roll(x, -16, 1), roll(x, 16, 1)
        carried = jnp.where(sub_index() == 7, roll(ahead, -1, 0), roll(behind, -1, 0))
        return jnp.where(lane_index() % 32 < 16, ahead, carried)
    if d == -1:
        ahead, behind = roll(x, -16, 1), roll(x, 16, 1)
        carried = jnp.where(sub_index() == 0, roll(behind, 1, 0), roll(ahead, 1, 0))
        return jnp.where(lane_index() % 32 < 16, carried, behind)
    e = d // 2
    moved = roll(x, -e, 0)
    crossed = sub_index() >= 8 - e if e > 0 else sub_index() < -e
    return jnp.where(crossed, roll(moved, -32 if e > 0 else 32, 1), moved)


def axl_from(x, d):
    return roll(x, -d, 0)


def rad_from(x, d):
    if abs(d) >= 8:
        return roll(x, 64, 1)
    moved = roll(x, -d, 0)
    crossed = sub_index() >= 8 - d if d > 0 else sub_index() < -d
    return jnp.where(crossed, roll(moved, 64, 1), moved)


def factor(m):
    m = [list(row) for row in m]
    inv = []
    for k in range(N):
        inv.append(1.0 / m[k][k])
        for i in range(k + 1, N):
            m[i][k] = m[i][k] * inv[k]
            for j in range(k + 1, N):
                m[i][j] = m[i][j] - m[i][k] * m[k][j]
    return m, inv


def factored_solve(m, inv, b):
    b = list(b)
    for i in range(N):
        for j in range(i):
            b[i] = b[i] - m[i][j] * b[j]
    for i in reversed(range(N)):
        for j in range(i + 1, N):
            b[i] = b[i] - m[i][j] * b[j]
        b[i] = b[i] * inv[i]
    return b


def times(m, v):
    out = []
    for i in range(N):
        acc = m[i][0] * v[0]
        for j in range(1, N):
            acc = acc + m[i][j] * v[j]
        out.append(acc)
    return out


def add(a, b):
    return [x + y for x, y in zip(a, b)]


def sub(a, b):
    return [x - y for x, y in zip(a, b)]


class LineSolver:
    def __init__(self, mats, direction, neighbour, shifts, first, last, store):
        self.hats, self.links, self.factors, self.face = store
        self.neighbour, self.shifts, self.first, self.last = neighbour, shifts, first, last
        convection = [[mats[direction, i, 0, j] for j in range(N)] for i in range(N)]
        self.reaction = [[mats[direction, i, 1, j] for j in range(N)] for i in range(N)]
        unit = [[1.0 if i == j else 0.0 for j in range(N)] for i in range(N)]
        self.plus = [[unit[i][j] + convection[i][j] for j in range(N)] for i in range(N)]
        self.minus = [[unit[i][j] - convection[i][j] for j in range(N)] for i in range(N)]

    def built_links(self, r):
        link_lo, link_hi = self.face[r], self.face[r + 1]
        if self.first is not None:
            link_lo = jnp.where(self.first & (r == 0), 0.0, link_lo)
            link_hi = jnp.where(self.last & (r == 7), 0.0, link_hi)
        lower = [[link_lo * self.plus[i][j] for j in range(N)] for i in range(N)]
        upper = [[link_hi * self.minus[i][j] for j in range(N)] for i in range(N)]
        return lower, upper

    def built_diag(self, r, source):
        middle = 1.0 + self.face[r] + self.face[r + 1]
        return [
            [
                source * self.reaction[i][j] + middle if i == j else source * self.reaction[i][j]
                for j in range(N)
            ]
            for i in range(N)
        ]

    def matrix(self, ref, slot, start):
        cols = [[ref[slot, (start + j) * N + i] for i in range(N)] for j in range(N)]
        return [[cols[j][i] for j in range(N)] for i in range(N)]

    def put(self, ref, slot, col, values):
        for i in range(N):
            ref[slot, col * N + i] = values[i]

    def keep_factor(self, slot, diag):
        m, inv = factor(diag)
        for i in range(N):
            for j in range(N):
                self.factors[slot, i * N + j] = inv[i] if i == j else m[i][j]
        return m, inv

    def solved(self, slot, right):
        m = [[self.factors[slot, i * N + j] for j in range(N)] for i in range(N)]
        return factored_solve(m, [m[i][i] for i in range(N)], right)

    def hat_column(self, slot, col):
        return [self.hats[slot, col * N + i] for i in range(N)]

    def prepare(self, coeff, source):
        neighbour, face, first = self.neighbour, self.face, self.first
        hats, links = self.hats, self.links
        before, after = neighbour(coeff[7], -1), neighbour(coeff[0], 1)
        if first is not None:
            before = jnp.where(first, 0.0, before)
            after = jnp.where(self.last, 0.0, after)
        face[0] = 0.5 * (before + coeff[0])
        face[8] = 0.5 * (coeff[7] + after)
        for r in range(1, 8):
            face[r] = 0.5 * (coeff[r - 1] + coeff[r])

        def normalise(slot, kept, diag, column):
            m, inv = self.keep_factor(kept, diag)
            for col in range(10):
                self.put(hats, slot, col, factored_solve(m, inv, column(col)))

        def normalise_built(r, kept):
            lower, upper = self.built_links(r)
            both = [lower, upper]
            normalise(
                r, kept, self.built_diag(r, source[r]),
                lambda col: [both[col // N][i][col % N] for i in range(N)],
            )

        def normalise_kept(slot, row, kept):
            normalise(
                slot, kept, self.matrix(links, row, DIAG),
                lambda col: [links[row, col * N + i] for i in range(N)],
            )

        def combine(target, diag, lower, upper, prev, following, want_links=True):
            acc = []
            for j in range(N):
                if want_links:
                    self.put(links, target, LOWER + j, times(lower, prev(LOWER + j)))
                acc.append(sub([diag[i][j] for i in range(N)], times(lower, prev(UPPER + j))))
            for j in range(N):
                if want_links:
                    self.put(links, target, UPPER + j, times(upper, following(UPPER + j)))
                self.put(
                    links, target, DIAG + j, sub(acc[j], times(upper, following(LOWER + j)))
                )

        def combine_kept(target, row, below, above):
            combine(
                target, self.matrix(links, row, DIAG), self.matrix(links, row, LOWER),
                self.matrix(links, row, UPPER), lambda col: self.hat_column(below, col),
                lambda col: self.hat_column(above, col),
            )

        def borrow(slot, r):
            def one(q, _):
                hats[slot, q] = neighbour(hats[r, q], 1)
                return 0

            lax.fori_loop(0, 10 * N, one, 0, unroll=10)

        @pl.loop(0, 4)
        def _(k):
            normalise_built(2 * k, k)

        borrow(8, 0)

        @pl.loop(0, 4)
        def _(k):
            r = 2 * k + 1
            lower, upper = self.built_links(r)
            combine(
                r, self.built_diag(r, source[r]), lower, upper,
                lambda col: self.hat_column(r - 1, col), lambda col: self.hat_column(r + 1, col),
            )

        @pl.loop(0, 2)
        def _(k):
            normalise_kept(4 * k + 1, 4 * k + 1, 4 + k)

        borrow(9, 1)

        @pl.loop(0, 2)
        def _(k):
            combine_kept(8 + k, 4 * k + 3, 4 * k + 1, 4 * k + 5)

        normalise_kept(3, 8, 6)
        borrow(11, 3)
        combine_kept(10, 9, 3, 11)
        for k, d in enumerate(self.shifts):
            row = 10 + k
            normalise_kept(7, row, 7 + k)
            combine(
                row + 1, self.matrix(links, row, DIAG), self.matrix(links, row, LOWER),
                self.matrix(links, row, UPPER),
                lambda col: [neighbour(v, -d) for v in self.hat_column(7, col)],
                lambda col: [neighbour(v, d) for v in self.hat_column(7, col)],
                want_links=first is None or d != self.shifts[-1],
            )
        row = 10 + len(self.shifts)
        diag = self.matrix(links, row, DIAG)
        if first is None:
            lower, upper = self.matrix(links, row, LOWER), self.matrix(links, row, UPPER)
            diag = [[diag[i][j] - lower[i][j] - upper[i][j] for j in range(N)] for i in range(N)]
        self.keep_factor(7 + len(self.shifts), diag)

    def finish(self, right, out):
        neighbour, links = self.neighbour, self.links

        def gather(r, lower, upper, below, above):
            return add(add(r, times(lower, below)), times(upper, above))

        def kept(row):
            return self.matrix(links, row, LOWER), self.matrix(links, row, UPPER)

        def shifted(values, d):
            return [neighbour(v, d) for v in values]

        def load(r):
            return [right[i, r] for i in range(N)]

        hat = {r: self.solved(r // 2, load(r)) for r in (0, 2, 4, 6)}
        hat[8] = shifted(hat[0], 1)
        rhs = {
            r: gather(load(r), *self.built_links(r), hat[r - 1], hat[r + 1]) for r in (1, 3, 5, 7)
        }
        hat[1], hat[5] = self.solved(4, rhs[1]), self.solved(5, rhs[5])
        rhs[3] = gather(rhs[3], *kept(3), hat[1], hat[5])
        rhs[7] = gather(rhs[7], *kept(7), hat[5], shifted(hat[1], 1))
        hat[3] = self.solved(6, rhs[3])
        last = gather(rhs[7], *kept(9), hat[3], shifted(hat[3], 1))
        for k, d in enumerate(self.shifts):
            part = self.solved(7 + k, last)
            last = gather(last, *kept(10 + k), shifted(part, -d), shifted(part, d))
        x = {7: self.solved(7 + len(self.shifts), last)}
        x[-1] = shifted(x[7], -1)

        def settle(r, step):
            lower = self.matrix(self.hats, r, LOWER)
            upper = self.matrix(self.hats, r, UPPER)
            x[r] = gather(hat[r], lower, upper, x[r - step], x[r + step])

        for r, step in ((3, 4), (1, 2), (5, 2), (0, 1), (2, 1), (4, 1), (6, 1)):
            settle(r, step)
        for r in range(8):
            for i in range(N):
                out[i, r] = x[r][i]


def swap_blocks(values):
    values = list(values)
    count = len(values)
    width = 128 // count
    bit = 1
    while bit < count:
        upper = (lane_index() // (bit * width)) % 2 == 1
        for a in range(count):
            if a & bit == 0:
                lo, hi = values[a], values[a | bit]
                values[a] = jnp.where(upper, roll(hi, bit * width, 1), lo)
                values[a | bit] = jnp.where(upper, hi, roll(lo, -bit * width, 1))
        bit *= 2
    return values


class Exchange:
    def __init__(self, axis, count, send, recv, start, rows, pitch, send_sem, recv_sem):
        self.axis, self.count, self.offset = axis, count, start
        self.rows, self.pitch = rows, pitch
        self.send, self.recv = send, recv
        self.send_sem, self.recv_sem = send_sem, recv_sem
        self.me = lax.axis_index(axis)

    def slot(self, ref, device):
        return ref.at[pl.ds(pl.multiple_of(device * self.pitch + self.offset, 8), self.rows)]

    def copy(self, k):
        target = lax.rem(self.me + k, self.count)
        return pltpu.make_async_remote_copy(
            src_ref=self.slot(self.send, target),
            dst_ref=self.slot(self.recv, self.me),
            send_sem=self.send_sem.at[k],
            recv_sem=self.recv_sem.at[k],
            device_id={self.axis: target},
            device_id_type=pl.DeviceIdType.MESH,
        )

    def start(self):
        @pl.loop(1, self.count)
        def _(k):
            self.copy(k).start()

        own = pl.ds(pl.multiple_of(self.me * self.pitch + self.offset, 8), self.rows)
        self.recv[own, :] = self.send[own, :]

    def wait_recv(self):
        @pl.loop(1, self.count)
        def _(k):
            self.copy(k).wait_recv()

    def wait_send(self):
        @pl.loop(1, self.count)
        def _(k):
            self.copy(k).wait_send()


def kernel(
    mats, explicit_in, diffusion_in, source_in, out,
    explicit, diffusion, source_rate,
    tiles, staged, a_send, a_recv, b_send, b_recv, k_send, k_recv, c_send, c_recv, o_send, o_recv,
    fields, mid, planes, hats, links, factors, face, load_sems, azi_sems, axl_sems,
):
    loads = [
        pltpu.make_async_copy(source, target, load_sems.at[n])
        for n, (source, target) in enumerate(
            ((diffusion_in, diffusion), (source_in, source_rate), (explicit_in, explicit))
        )
    ]
    for load in loads:
        load.start()

    barrier = pltpu.get_barrier_semaphore()
    for axis, count in (("azi", 32), ("axl", 16)):
        position = lax.axis_index(axis)

        @pl.loop(1, count)
        def _(k):
            pl.semaphore_signal(
                barrier, inc=1, device_id={axis: lax.rem(position + k, count)},
                device_id_type=pl.DeviceIdType.MESH,
            )

    lines_coeffs = Exchange("azi", 32, a_send, a_recv, 0, 4, 24, azi_sems.at[4], azi_sems.at[5])
    lines_out = Exchange("azi", 32, a_send, a_recv, 8, 10, 24, azi_sems.at[0], azi_sems.at[1])
    lines_back = Exchange("azi", 32, b_send, b_recv, 0, 10, 16, azi_sems.at[2], azi_sems.at[3])
    coeffs_out = Exchange("axl", 16, k_send, k_recv, 0, 12, 16, axl_sems.at[0], axl_sems.at[1])
    plane_out = Exchange("axl", 16, c_send, c_recv, 0, 20, 24, axl_sems.at[2], axl_sems.at[3])
    plane_back = Exchange("axl", 16, o_send, o_recv, 0, 20, 24, axl_sems.at[4], axl_sems.at[5])

    low_half = lane_index() < 64

    def store(k):
        return hats.at[k], links.at[k], factors.at[k], face.at[k]

    azimuthal = LineSolver(mats, 0, azi_from, (1, 2, 4, 8, 16, 32), None, None, store(0))
    axial = LineSolver(
        mats, 1, axl_from, (1, 2, 4), sub_index() == 0, sub_index() == 7, store(1)
    )
    radial = LineSolver(
        mats, 2, rad_from, (1, 2, 4, 8), (sub_index() == 0) & low_half,
        (sub_index() == 7) & jnp.logical_not(low_half), store(0),
    )

    def stage(f, place, part):
        for m in range(8):
            for half in range(2):
                i = (m % 2) * 8 + half * 4 + m // 2
                tiles[f, m, pl.ds(half * 4, 4), :] = part(i)
        for b, value in enumerate(swap_blocks([tiles[f, m] for m in range(8)])):
            staged[b, pl.ds(place, 8), :] = value

    loads[0].wait()
    loads[1].wait()
    stage(5, 0, lambda i: diffusion[0, i])
    stage(6, 8, lambda i: source_rate[i])
    for b in range(8):
        for j in range(4):
            a_send[pl.ds((j * 8 + b) * 24, 4), :] = staged[b, pl.ds(j, 4, stride=4), :]

    pl.semaphore_wait(barrier, 46)
    lines_coeffs.start()

    loads[2].wait()
    for f in range(5):
        stage(f, 16 + f * 8, lambda i: explicit[f, i])
    for b in range(8):
        for j in range(4):
            a_send[pl.ds((j * 8 + b) * 24 + 8, 10), :] = staged[b, pl.ds(16 + j, 10, stride=4), :]
    lines_out.start()

    for i in range(16):
        for f, part in enumerate((diffusion[1, i], diffusion[2, i], source_rate[i])):
            k_send[pl.ds(i * 16 + f * 4, 4), :] = part
    coeffs_out.start()

    def take_lines(f, row):
        for half in range(2):
            got = [a_recv[pl.ds(t * 192 + row + half, 8, stride=24), :] for t in range(4)]
            for k, value in enumerate(swap_blocks(got)):
                fields[f, half * 4 + k] = value

    lines_coeffs.wait_recv()
    take_lines(5, 0)
    take_lines(6, 2)
    azimuthal.prepare(fields.at[5], fields.at[6])
    lines_out.wait_recv()
    for f in range(5):
        take_lines(f, 8 + 2 * f)
    azimuthal.finish(fields, mid)

    for f in range(5):
        for half in range(2):
            values = swap_blocks([mid[f, half * 4 + k] for k in range(4)])
            for t in range(4):
                b_send[pl.ds(t * 128 + f * 2 + half, 8, stride=16), :] = values[t]
    lines_back.start()

    def axial_rows(r, f, pitch):
        return pl.ds((r // 4) * pitch + f * 4 + r % 4, 8, stride=2 * pitch)

    coeffs_out.wait_recv()
    for r in range(8):
        fields[5, r] = k_recv[axial_rows(r, 0, 16), :]
        fields[6, r] = k_recv[axial_rows(r, 2, 16), :]
    axial.prepare(fields.at[5], fields.at[6])

    lines_back.wait_recv()
    for f in range(5):
        for b in range(8):
            for half in range(2):
                tiles[f, b, pl.ds(half * 4, 4), :] = b_recv[
                    pl.ds(b * 16 + f * 2 + half, 4, stride=128), :
                ]
        for m, value in enumerate(swap_blocks([tiles[f, b] for b in range(8)])):
            tiles[f, m] = value
        for m in range(8):
            for half in range(2):
                i = (m % 2) * 8 + half * 4 + m // 2
                c_send[pl.ds(i * 24 + f * 4, 4), :] = tiles[f, m, pl.ds(half * 4, 4), :]
    plane_out.start()

    def turned(plane):
        flat = plane.reshape(64, 128).T
        return jnp.concatenate([flat[:64], flat[64:]], axis=1)

    def turn_rows(f):
        for r in range(8):
            fields[f, r] = planes[f, pl.ds(r, 8, stride=8), :]

    planes[6] = turned(fields[6])
    for r in range(8):
        fields[5, r] = k_recv[axial_rows(r, 1, 16), :]
    planes[5] = turned(fields[5])
    turn_rows(5)
    turn_rows(6)
    radial.prepare(fields.at[5], fields.at[6])

    plane_out.wait_recv()
    for r in range(8):
        for f in range(5):
            fields[f, r] = c_recv[axial_rows(r, f, 24), :]
    axial.finish(fields, mid)
    for f in range(5):
        planes[f] = turned(mid[f])
        turn_rows(f)
    radial.finish(fields, mid)
    for f in range(5):
        for r in range(8):
            planes[f, pl.ds(r, 8, stride=8), :] = mid[f, r]
        both = planes[f]
        mid[f] = jnp.concatenate([both[:, :64], both[:, 64:]], axis=0).T.reshape(8, 8, 128)
        for r in range(8):
            o_send[axial_rows(r, f, 24), :] = mid[f, r]
    plane_back.start()
    plane_back.wait_recv()
    for f in range(5):
        for i in range(16):
            out[f, i] = o_recv[pl.ds(i * 24 + f * 4, 4), :]
    for exchange in (lines_coeffs, lines_out, lines_back, coeffs_out, plane_out, plane_back):
        exchange.wait_send()


IN_VMEM = pl.BlockSpec(memory_space=pltpu.VMEM)
IN_SMEM = pl.BlockSpec(memory_space=pltpu.SMEM)


def body(explicit_residual, diffusion, source_rate, line_mats):
    return pl.pallas_call(
        kernel,
        out_shape=jax.ShapeDtypeStruct((5, 16, 4, 128), jnp.float32),
        in_specs=[IN_SMEM] + [pl.BlockSpec(memory_space=pl.ANY)] * 3,
        out_specs=IN_VMEM,
        scratch_shapes=[
            pltpu.VMEM((5, 16, 4, 128), jnp.float32),
            pltpu.VMEM((3, 16, 4, 128), jnp.float32),
            pltpu.VMEM((16, 4, 128), jnp.float32),
            pltpu.VMEM((7, 8, 8, 128), jnp.float32),
            pltpu.VMEM((8, 64, 128), jnp.float32),
            pltpu.VMEM((768, 128), jnp.float32),
            pltpu.VMEM((768, 128), jnp.float32),
            pltpu.VMEM((512, 128), jnp.float32),
            pltpu.VMEM((512, 128), jnp.float32),
            pltpu.VMEM((256, 128), jnp.float32),
            pltpu.VMEM((256, 128), jnp.float32),
            pltpu.VMEM((384, 128), jnp.float32),
            pltpu.VMEM((384, 128), jnp.float32),
            pltpu.VMEM((384, 128), jnp.float32),
            pltpu.VMEM((384, 128), jnp.float32),
            pltpu.VMEM((7, 8, 8, 128), jnp.float32),
            pltpu.VMEM((5, 8, 8, 128), jnp.float32),
            pltpu.VMEM((7, 64, 128), jnp.float32),
            pltpu.VMEM((2, 12, 50, 8, 128), jnp.float32),
            pltpu.VMEM((2, 17, 75, 8, 128), jnp.float32),
            pltpu.VMEM((2, 14, 25, 8, 128), jnp.float32),
            pltpu.VMEM((2, 9, 8, 128), jnp.float32),
            pltpu.SemaphoreType.DMA((3,)),
            pltpu.SemaphoreType.DMA((6, 32)),
            pltpu.SemaphoreType.DMA((6, 16)),
        ],
        compiler_params=pltpu.CompilerParams(
            collective_id=0, has_side_effects=True, vmem_limit_bytes=56 * 1024 * 1024
        ),
        cost_estimate=pl.CostEstimate(
            flops=120000000, bytes_accessed=600000, transcendentals=0
        ),
    )(line_mats.transpose(0, 2, 1, 3), explicit_residual, diffusion, source_rate)


def solution(mesh):
    in_specs = (
        P(None, "azi", "axl", None),
        P(None, "azi", "axl", None),
        P("azi", "axl", None),
        P(),
    )
    out_specs = P(None, "azi", "axl", None)
    return jax.shard_map(body, mesh=mesh, in_specs=in_specs, out_specs=out_specs, check_vma=False)
```

```python
import jax
import jax.numpy as jnp
from jax import lax
from jax.experimental import pallas as pl
from jax.experimental.pallas import tpu as pltpu
from jax.sharding import PartitionSpec as P

N = 5
LOWER, UPPER, DIAG = 0, 5, 10


def lane_index():
    return lax.broadcasted_iota(jnp.int32, (8, 128), 1)


def sub_index():
    return lax.broadcasted_iota(jnp.int32, (8, 128), 0)


def roll(x, shift, axis):
    size = 8 if axis == 0 else 128
    return pltpu.roll(x, shift % size, axis)


def azi_from(x, d):
    if abs(d) >= 16:
        return roll(x, -2 * d, 1)
    if d == 1:
        ahead, behind = roll(x, -16, 1), roll(x, 16, 1)
        carried = jnp.where(sub_index() == 7, roll(ahead, -1, 0), roll(behind, -1, 0))
        return jnp.where(lane_index() % 32 < 16, ahead, carried)
    if d == -1:
        ahead, behind = roll(x, -16, 1), roll(x, 16, 1)
        carried = jnp.where(sub_index() == 0, roll(behind, 1, 0), roll(ahead, 1, 0))
        return jnp.where(lane_index() % 32 < 16, carried, behind)
    e = d // 2
    moved = roll(x, -e, 0)
    crossed = sub_index() >= 8 - e if e > 0 else sub_index() < -e
    return jnp.where(crossed, roll(moved, -32 if e > 0 else 32, 1), moved)


def axl_from(x, d):
    return roll(x, -d, 0)


def rad_from(x, d):
    if abs(d) >= 8:
        return roll(x, 64, 1)
    moved = roll(x, -d, 0)
    crossed = sub_index() >= 8 - d if d > 0 else sub_index() < -d
    return jnp.where(crossed, roll(moved, 64, 1), moved)


def factor(m):
    m = [list(row) for row in m]
    inv = []
    for k in range(N):
        inv.append(1.0 / m[k][k])
        for i in range(k + 1, N):
            m[i][k] = m[i][k] * inv[k]
            for j in range(k + 1, N):
                m[i][j] = m[i][j] - m[i][k] * m[k][j]
    return m, inv


def factored_solve(m, inv, b):
    b = list(b)
    for i in range(N):
        for j in range(i):
            b[i] = b[i] - m[i][j] * b[j]
    for i in reversed(range(N)):
        for j in range(i + 1, N):
            b[i] = b[i] - m[i][j] * b[j]
        b[i] = b[i] * inv[i]
    return b


def times(m, v):
    out = []
    for i in range(N):
        acc = m[i][0] * v[0]
        for j in range(1, N):
            acc = acc + m[i][j] * v[j]
        out.append(acc)
    return out


def add(a, b):
    return [x + y for x, y in zip(a, b)]


def sub(a, b):
    return [x - y for x, y in zip(a, b)]


class LineSolver:
    def __init__(self, mats, direction, neighbour, shifts, first, last, store):
        self.hats, self.links, self.factors, self.face = store
        self.neighbour, self.shifts, self.first, self.last = neighbour, shifts, first, last
        convection = [[mats[direction, i, 0, j] for j in range(N)] for i in range(N)]
        self.reaction = [[mats[direction, i, 1, j] for j in range(N)] for i in range(N)]
        unit = [[1.0 if i == j else 0.0 for j in range(N)] for i in range(N)]
        self.plus = [[unit[i][j] + convection[i][j] for j in range(N)] for i in range(N)]
        self.minus = [[unit[i][j] - convection[i][j] for j in range(N)] for i in range(N)]

    def built_links(self, r):
        link_lo, link_hi = self.face[r], self.face[r + 1]
        if self.first is not None:
            link_lo = jnp.where(self.first & (r == 0), 0.0, link_lo)
            link_hi = jnp.where(self.last & (r == 7), 0.0, link_hi)
        lower = [[link_lo * self.plus[i][j] for j in range(N)] for i in range(N)]
        upper = [[link_hi * self.minus[i][j] for j in range(N)] for i in range(N)]
        return lower, upper

    def built_diag(self, r, source):
        middle = 1.0 + self.face[r] + self.face[r + 1]
        return [
            [
                source * self.reaction[i][j] + middle if i == j else source * self.reaction[i][j]
                for j in range(N)
            ]
            for i in range(N)
        ]

    def matrix(self, ref, slot, start):
        cols = [[ref[slot, (start + j) * N + i] for i in range(N)] for j in range(N)]
        return [[cols[j][i] for j in range(N)] for i in range(N)]

    def put(self, ref, slot, col, values):
        for i in range(N):
            ref[slot, col * N + i] = values[i]

    def keep_factor(self, slot, diag):
        m, inv = factor(diag)
        for i in range(N):
            for j in range(N):
                self.factors[slot, i * N + j] = inv[i] if i == j else m[i][j]
        return m, inv

    def solved(self, slot, right):
        m = [[self.factors[slot, i * N + j] for j in range(N)] for i in range(N)]
        return factored_solve(m, [m[i][i] for i in range(N)], right)

    def hat_column(self, slot, col):
        return [self.hats[slot, col * N + i] for i in range(N)]

    def prepare(self, coeff, source):
        neighbour, face, first = self.neighbour, self.face, self.first
        hats, links = self.hats, self.links
        before, after = neighbour(coeff[7], -1), neighbour(coeff[0], 1)
        if first is not None:
            before = jnp.where(first, 0.0, before)
            after = jnp.where(self.last, 0.0, after)
        face[0] = 0.5 * (before + coeff[0])
        face[8] = 0.5 * (coeff[7] + after)
        for r in range(1, 8):
            face[r] = 0.5 * (coeff[r - 1] + coeff[r])

        def normalise(slot, kept, diag, column):
            m, inv = self.keep_factor(kept, diag)
            for col in range(10):
                self.put(hats, slot, col, factored_solve(m, inv, column(col)))

        def normalise_built(r, kept):
            lower, upper = self.built_links(r)
            both = [lower, upper]
            normalise(
                r, kept, self.built_diag(r, source[r]),
                lambda col: [both[col // N][i][col % N] for i in range(N)],
            )

        def normalise_kept(slot, row, kept):
            normalise(
                slot, kept, self.matrix(links, row, DIAG),
                lambda col: [links[row, col * N + i] for i in range(N)],
            )

        def combine(target, diag, lower, upper, prev, following, want_links=True):
            acc = []
            for j in range(N):
                if want_links:
                    self.put(links, target, LOWER + j, times(lower, prev(LOWER + j)))
                acc.append(sub([diag[i][j] for i in range(N)], times(lower, prev(UPPER + j))))
            for j in range(N):
                if want_links:
                    self.put(links, target, UPPER + j, times(upper, following(UPPER + j)))
                self.put(
                    links, target, DIAG + j, sub(acc[j], times(upper, following(LOWER + j)))
                )

        def combine_kept(target, row, below, above):
            combine(
                target, self.matrix(links, row, DIAG), self.matrix(links, row, LOWER),
                self.matrix(links, row, UPPER), lambda col: self.hat_column(below, col),
                lambda col: self.hat_column(above, col),
            )

        def borrow(slot, r):
            def one(q, _):
                hats[slot, q] = neighbour(hats[r, q], 1)
                return 0

            lax.fori_loop(0, 10 * N, one, 0, unroll=10)

        @pl.loop(0, 4)
        def _(k):
            normalise_built(2 * k, k)

        borrow(8, 0)

        @pl.loop(0, 4)
        def _(k):
            r = 2 * k + 1
            lower, upper = self.built_links(r)
            combine(
                r, self.built_diag(r, source[r]), lower, upper,
                lambda col: self.hat_column(r - 1, col), lambda col: self.hat_column(r + 1, col),
            )

        @pl.loop(0, 2)
        def _(k):
            normalise_kept(4 * k + 1, 4 * k + 1, 4 + k)

        borrow(9, 1)

        @pl.loop(0, 2)
        def _(k):
            combine_kept(8 + k, 4 * k + 3, 4 * k + 1, 4 * k + 5)

        normalise_kept(3, 8, 6)
        borrow(11, 3)
        combine_kept(10, 9, 3, 11)
        for k, d in enumerate(self.shifts):
            row = 10 + k
            normalise_kept(7, row, 7 + k)
            combine(
                row + 1, self.matrix(links, row, DIAG), self.matrix(links, row, LOWER),
                self.matrix(links, row, UPPER),
                lambda col: [neighbour(v, -d) for v in self.hat_column(7, col)],
                lambda col: [neighbour(v, d) for v in self.hat_column(7, col)],
                want_links=first is None or d != self.shifts[-1],
            )
        row = 10 + len(self.shifts)
        diag = self.matrix(links, row, DIAG)
        if first is None:
            lower, upper = self.matrix(links, row, LOWER), self.matrix(links, row, UPPER)
            diag = [[diag[i][j] - lower[i][j] - upper[i][j] for j in range(N)] for i in range(N)]
        self.keep_factor(7 + len(self.shifts), diag)

    def finish(self, right, out):
        neighbour, links = self.neighbour, self.links

        def gather(r, lower, upper, below, above):
            return add(add(r, times(lower, below)), times(upper, above))

        def kept(row):
            return self.matrix(links, row, LOWER), self.matrix(links, row, UPPER)

        def shifted(values, d):
            return [neighbour(v, d) for v in values]

        def load(r):
            return [right[i, r] for i in range(N)]

        hat = {r: self.solved(r // 2, load(r)) for r in (0, 2, 4, 6)}
        hat[8] = shifted(hat[0], 1)
        rhs = {
            r: gather(load(r), *self.built_links(r), hat[r - 1], hat[r + 1]) for r in (1, 3, 5, 7)
        }
        hat[1], hat[5] = self.solved(4, rhs[1]), self.solved(5, rhs[5])
        rhs[3] = gather(rhs[3], *kept(3), hat[1], hat[5])
        rhs[7] = gather(rhs[7], *kept(7), hat[5], shifted(hat[1], 1))
        hat[3] = self.solved(6, rhs[3])
        last = gather(rhs[7], *kept(9), hat[3], shifted(hat[3], 1))
        for k, d in enumerate(self.shifts):
            part = self.solved(7 + k, last)
            last = gather(last, *kept(10 + k), shifted(part, -d), shifted(part, d))
        x = {7: self.solved(7 + len(self.shifts), last)}
        x[-1] = shifted(x[7], -1)

        def settle(r, step):
            lower = self.matrix(self.hats, r, LOWER)
            upper = self.matrix(self.hats, r, UPPER)
            x[r] = gather(hat[r], lower, upper, x[r - step], x[r + step])

        for r, step in ((3, 4), (1, 2), (5, 2), (0, 1), (2, 1), (4, 1), (6, 1)):
            settle(r, step)
        for r in range(8):
            for i in range(N):
                out[i, r] = x[r][i]


def swap_blocks(values):
    values = list(values)
    count = len(values)
    width = 128 // count
    bit = 1
    while bit < count:
        upper = (lane_index() // (bit * width)) % 2 == 1
        for a in range(count):
            if a & bit == 0:
                lo, hi = values[a], values[a | bit]
                values[a] = jnp.where(upper, roll(hi, bit * width, 1), lo)
                values[a | bit] = jnp.where(upper, hi, roll(lo, -bit * width, 1))
        bit *= 2
    return values


class Exchange:
    def __init__(self, axis, count, send, recv, start, rows, pitch, send_sem, recv_sem):
        self.axis, self.count, self.offset = axis, count, start
        self.rows, self.pitch = rows, pitch
        self.send, self.recv = send, recv
        self.send_sem, self.recv_sem = send_sem, recv_sem
        self.me = lax.axis_index(axis)

    def slot(self, ref, device):
        return ref.at[pl.ds(pl.multiple_of(device * self.pitch + self.offset, 8), self.rows)]

    def copy(self, k):
        target = lax.rem(self.me + k, self.count)
        return pltpu.make_async_remote_copy(
            src_ref=self.slot(self.send, target),
            dst_ref=self.slot(self.recv, self.me),
            send_sem=self.send_sem.at[k],
            recv_sem=self.recv_sem.at[k],
            device_id={self.axis: target},
            device_id_type=pl.DeviceIdType.MESH,
        )

    def start(self):
        @pl.loop(1, self.count)
        def _(k):
            self.copy(k).start()

        own = pl.ds(pl.multiple_of(self.me * self.pitch + self.offset, 8), self.rows)
        self.recv[own, :] = self.send[own, :]

    def wait_recv(self):
        @pl.loop(1, self.count)
        def _(k):
            self.copy(k).wait_recv()

    def wait_send(self):
        @pl.loop(1, self.count)
        def _(k):
            self.copy(k).wait_send()


def kernel(
    mats, explicit, diffusion, source_rate, out,
    tiles, staged, a_send, a_recv, b_send, b_recv, k_send, k_recv, c_send, c_recv, o_send, o_recv,
    fields, mid, planes, hats, links, factors, face, azi_sems, axl_sems,
):
    barrier = pltpu.get_barrier_semaphore()
    for axis, count in (("azi", 32), ("axl", 16)):
        position = lax.axis_index(axis)

        @pl.loop(1, count)
        def _(k):
            pl.semaphore_signal(
                barrier, inc=1, device_id={axis: lax.rem(position + k, count)},
                device_id_type=pl.DeviceIdType.MESH,
            )

    lines_coeffs = Exchange("azi", 32, a_send, a_recv, 0, 4, 24, azi_sems.at[4], azi_sems.at[5])
    lines_out = Exchange("azi", 32, a_send, a_recv, 8, 10, 24, azi_sems.at[0], azi_sems.at[1])
    lines_back = Exchange("azi", 32, b_send, b_recv, 0, 10, 16, azi_sems.at[2], azi_sems.at[3])
    coeffs_out = Exchange("axl", 16, k_send, k_recv, 0, 12, 16, axl_sems.at[0], axl_sems.at[1])
    plane_out = Exchange("axl", 16, c_send, c_recv, 0, 20, 24, axl_sems.at[2], axl_sems.at[3])
    plane_back = Exchange("axl", 16, o_send, o_recv, 0, 20, 24, axl_sems.at[4], axl_sems.at[5])

    low_half = lane_index() < 64

    def store(k):
        return hats.at[k], links.at[k], factors.at[k], face.at[k]

    azimuthal = LineSolver(mats, 0, azi_from, (1, 2, 4, 8, 16, 32), None, None, store(0))
    axial = LineSolver(
        mats, 1, axl_from, (1, 2, 4), sub_index() == 0, sub_index() == 7, store(1)
    )
    radial = LineSolver(
        mats, 2, rad_from, (1, 2, 4, 8), (sub_index() == 0) & low_half,
        (sub_index() == 7) & jnp.logical_not(low_half), store(0),
    )

    def stage(f, place, part):
        for m in range(8):
            for half in range(2):
                i = (m % 2) * 8 + half * 4 + m // 2
                tiles[f, m, pl.ds(half * 4, 4), :] = part(i)
        for b, value in enumerate(swap_blocks([tiles[f, m] for m in range(8)])):
            staged[b, pl.ds(place, 8), :] = value

    stage(5, 0, lambda i: diffusion[0, i])
    stage(6, 8, lambda i: source_rate[i])
    for b in range(8):
        for j in range(4):
            a_send[pl.ds((j * 8 + b) * 24, 4), :] = staged[b, pl.ds(j, 4, stride=4), :]

    pl.semaphore_wait(barrier, 46)
    lines_coeffs.start()

    for f in range(5):
        stage(f, 16 + f * 8, lambda i: explicit[f, i])
    for b in range(8):
        for j in range(4):
            a_send[pl.ds((j * 8 + b) * 24 + 8, 10), :] = staged[b, pl.ds(16 + j, 10, stride=4), :]
    lines_out.start()

    for i in range(16):
        for f, part in enumerate((diffusion[1, i], diffusion[2, i], source_rate[i])):
            k_send[pl.ds(i * 16 + f * 4, 4), :] = part
    coeffs_out.start()

    def take_lines(f, row):
        for half in range(2):
            got = [a_recv[pl.ds(t * 192 + row + half, 8, stride=24), :] for t in range(4)]
            for k, value in enumerate(swap_blocks(got)):
                fields[f, half * 4 + k] = value

    lines_coeffs.wait_recv()
    take_lines(5, 0)
    take_lines(6, 2)
    azimuthal.prepare(fields.at[5], fields.at[6])
    lines_out.wait_recv()
    for f in range(5):
        take_lines(f, 8 + 2 * f)
    azimuthal.finish(fields, mid)

    for f in range(5):
        for half in range(2):
            values = swap_blocks([mid[f, half * 4 + k] for k in range(4)])
            for t in range(4):
                b_send[pl.ds(t * 128 + f * 2 + half, 8, stride=16), :] = values[t]
    lines_back.start()

    def axial_rows(r, f, pitch):
        return pl.ds((r // 4) * pitch + f * 4 + r % 4, 8, stride=2 * pitch)

    coeffs_out.wait_recv()
    for r in range(8):
        fields[5, r] = k_recv[axial_rows(r, 0, 16), :]
        fields[6, r] = k_recv[axial_rows(r, 2, 16), :]
    axial.prepare(fields.at[5], fields.at[6])

    lines_back.wait_recv()
    for f in range(5):
        for b in range(8):
            for half in range(2):
                tiles[f, b, pl.ds(half * 4, 4), :] = b_recv[
                    pl.ds(b * 16 + f * 2 + half, 4, stride=128), :
                ]
        for m, value in enumerate(swap_blocks([tiles[f, b] for b in range(8)])):
            tiles[f, m] = value
        for m in range(8):
            for half in range(2):
                i = (m % 2) * 8 + half * 4 + m // 2
                c_send[pl.ds(i * 24 + f * 4, 4), :] = tiles[f, m, pl.ds(half * 4, 4), :]
    plane_out.start()

    def turned(plane):
        flat = plane.reshape(64, 128).T
        return jnp.concatenate([flat[:64], flat[64:]], axis=1)

    def turn_rows(f):
        for r in range(8):
            fields[f, r] = planes[f, pl.ds(r, 8, stride=8), :]

    planes[6] = turned(fields[6])
    for r in range(8):
        fields[5, r] = k_recv[axial_rows(r, 1, 16), :]
    planes[5] = turned(fields[5])
    turn_rows(5)
    turn_rows(6)
    radial.prepare(fields.at[5], fields.at[6])

    plane_out.wait_recv()
    for r in range(8):
        for f in range(5):
            fields[f, r] = c_recv[axial_rows(r, f, 24), :]
    axial.finish(fields, mid)
    for f in range(5):
        planes[f] = turned(mid[f])
        turn_rows(f)
    radial.finish(fields, mid)
    for f in range(5):
        for r in range(8):
            planes[f, pl.ds(r, 8, stride=8), :] = mid[f, r]
        both = planes[f]
        mid[f] = jnp.concatenate([both[:, :64], both[:, 64:]], axis=0).T.reshape(8, 8, 128)
        for r in range(8):
            o_send[axial_rows(r, f, 24), :] = mid[f, r]
    plane_back.start()
    plane_back.wait_recv()
    for f in range(5):
        for i in range(16):
            out[f, i] = o_recv[pl.ds(i * 24 + f * 4, 4), :]
    for exchange in (lines_coeffs, lines_out, lines_back, coeffs_out, plane_out, plane_back):
        exchange.wait_send()


IN_VMEM = pl.BlockSpec(memory_space=pltpu.VMEM)
IN_SMEM = pl.BlockSpec(memory_space=pltpu.SMEM)


def body(explicit_residual, diffusion, source_rate, line_mats):
    return pl.pallas_call(
        kernel,
        out_shape=jax.ShapeDtypeStruct((5, 16, 4, 128), jnp.float32),
        in_specs=[IN_SMEM, IN_VMEM, IN_VMEM, IN_VMEM],
        out_specs=IN_VMEM,
        scratch_shapes=[
            pltpu.VMEM((7, 8, 8, 128), jnp.float32),
            pltpu.VMEM((8, 64, 128), jnp.float32),
            pltpu.VMEM((768, 128), jnp.float32),
            pltpu.VMEM((768, 128), jnp.float32),
            pltpu.VMEM((512, 128), jnp.float32),
            pltpu.VMEM((512, 128), jnp.float32),
            pltpu.VMEM((256, 128), jnp.float32),
            pltpu.VMEM((256, 128), jnp.float32),
            pltpu.VMEM((384, 128), jnp.float32),
            pltpu.VMEM((384, 128), jnp.float32),
            pltpu.VMEM((384, 128), jnp.float32),
            pltpu.VMEM((384, 128), jnp.float32),
            pltpu.VMEM((7, 8, 8, 128), jnp.float32),
            pltpu.VMEM((5, 8, 8, 128), jnp.float32),
            pltpu.VMEM((7, 64, 128), jnp.float32),
            pltpu.VMEM((2, 12, 50, 8, 128), jnp.float32),
            pltpu.VMEM((2, 17, 75, 8, 128), jnp.float32),
            pltpu.VMEM((2, 14, 25, 8, 128), jnp.float32),
            pltpu.VMEM((2, 9, 8, 128), jnp.float32),
            pltpu.SemaphoreType.DMA((6, 32)),
            pltpu.SemaphoreType.DMA((6, 16)),
        ],
        compiler_params=pltpu.CompilerParams(
            collective_id=0, has_side_effects=True, vmem_limit_bytes=32 * 1024 * 1024
        ),
        cost_estimate=pl.CostEstimate(
            flops=120000000, bytes_accessed=600000, transcendentals=0
        ),
    )(line_mats.transpose(0, 2, 1, 3), explicit_residual, diffusion, source_rate)


def solution(mesh):
    in_specs = (
        P(None, "azi", "axl", None),
        P(None, "azi", "axl", None),
        P("azi", "axl", None),
        P(),
    )
    out_specs = P(None, "azi", "axl", None)
    return jax.shard_map(body, mesh=mesh, in_specs=in_specs, out_specs=out_specs, check_vma=False)
```
